32 devices in a mesh: grp: 8 (over z, core), fsdp: 4 (over y, x).
Axes of the slice: x: 2, y: 2, z: 4, core: 2. Of those that a mesh axis runs over, the one named last changes fastest.
Arguments:
- tokens: bfloat16 [32, 384, 1536], P(('grp', 'fsdp')), may hold values from -6 to 6
- doc_ids: int32 [32, 384], P(('grp', 'fsdp')), may hold values from 0 to 3, never falling along the last dimension, each value on 1 to 192 neighbouring positions
- cotangent: bfloat16 [32, 384, 1536], P(('grp', 'fsdp')), may hold values from -6 to 6
- gain_in: float32 [1536], P('fsdp'), may hold values from 0.5 to 1.5
- w_query: float32 [1536, 1536], P('fsdp'), may hold values from -0.15625 to 0.15625
- w_key: float32 [1536, 1536], P('fsdp'), may hold values from -0.15625 to 0.15625
- w_value: float32 [1536, 1536], P('fsdp'), may hold values from -0.15625 to 0.15625
- w_house: float32 [1536, 1536], P('fsdp'), may hold values from -0.15625 to 0.15625
- w_rate: float32 [1536, 12], P('fsdp'), may hold values from -0.15625 to 0.15625
- conv_taps: float32 [4, 1536], P(None, 'fsdp'), may hold values from -3 to 3
- w_out: float32 [1536, 1536], P('fsdp'), may hold values from -0.4375 to 0.4375
- gain_mid: float32 [1536], P('fsdp'), may hold values from 0.5 to 1.5
- w_gate: float32 [1536, 4096], P('fsdp'), may hold values from -0.15625 to 0.15625
- w_up: float32 [1536, 4096], P('fsdp'), may hold values from -0.15625 to 0.15625
- w_down: float32 [4096, 1536], P('fsdp'), may hold values from -0.09375 to 0.09375
Outputs:
- result: bfloat16 [32, 384, 1536], P(('grp', 'fsdp'))
- grad_tokens: float32 [32, 384, 1536], P(('grp', 'fsdp'))
- grad_gain_in: float32 [1536], P('fsdp')
- grad_query: float32 [1536, 1536], P('fsdp')
- grad_key: float32 [1536, 1536], P('fsdp')
- grad_value: float32 [1536, 1536], P('fsdp')
- grad_house: float32 [1536, 1536], P('fsdp')
- grad_rate: float32 [1536, 12], P('fsdp')
- grad_taps: float32 [4, 1536], P(None, 'fsdp')
- grad_out: float32 [1536, 1536], P('fsdp')
- grad_gain_mid: float32 [1536], P('fsdp')
- grad_gate: float32 [1536, 4096], P('fsdp')
- grad_up: float32 [1536, 4096], P('fsdp')
- grad_down: float32 [4096, 1536], P('fsdp')
The draws below stay inside these ranges and needn't reach their ends.
Inputs may be any that keep to these rules, and one draw needn't show every extreme that they name: `doc_ids`: within each row document numbers never fall, each of the 4 documents has 1 to 192 positions, and one has exactly 192.
All inputs are finite; a program needn't handle non-finite values.
Results may differ from the reference program's by a relative error of at most 0.025.
Values may be sent and summed in bfloat16 or wider, within the bound.
No kernel may reach another device: no remote copies, remote signals or barrier semaphores. Data moves between devices by JAX's collectives and lax.ppermute only.
A program may use at most 384 MiB of HBM per device.

```python
import math
import jax
import jax.numpy as jnp
import numpy as np
from jax import lax

D = 1536
HEADS = 12
FF = 4096
CONV = 4
DOCS = 4
ROW_LEN = 384
ROWS = 32


def level_of(rng, dims, split, least, largest):
    def one(dim, shards_of):
        draws = jax.random.uniform(jax.random.fold_in(jax.random.fold_in(rng, 6), dim), (shards_of,), jnp.float32, least / len(split), largest / len(split))
        return jnp.repeat(jnp.exp(draws), dims[dim] // shards_of).reshape((-1,) + (1,) * (len(dims) - dim - 1))

    level = one(*split[0])
    for cut in split[1:]:
        level = level * one(*cut)
    return level


def length_profile(count, total, most, lean):
    loads = [(1 << 20) // math.isqrt(grade ** lean) + 1 for grade in range(2, count + 1)]
    spare, holding = total - most - (count - 1), [1] * (count - 1)
    while spare > 0:
        free = [i for i in range(count - 1) if holding[i] < most]
        whole, budget = sum([loads[i] for i in free]), spare
        for i in free:
            more = min(most - holding[i], max(1, budget * loads[i] // whole), spare)
            holding[i] = holding[i] + more
            spare = spare - more
    return np.array([most] + holding)


def ragged_sizes(stream_key, amount, total, reach, skew):
    if amount == 2:
        one = jax.random.randint(stream_key, (), max(1, total - reach), min(reach, total - 1) + 1)
        return jnp.stack([one, total - one])
    sizes = jnp.asarray(length_profile(amount, total, reach, skew), jnp.int32)
    twos = (amount - 1) // 2
    giver, sink = sizes[1:1 + 2 * twos:2], sizes[2:2 + 2 * twos:2]
    slack = jnp.minimum(giver - 1, reach - sink)
    moved = jax.random.randint(jax.random.fold_in(stream_key, 1), (twos,), 0, 1 << 20) % (slack + 1)
    sizes = sizes.at[1:1 + 2 * twos:2].set(giver - moved).at[2:2 + 2 * twos:2].set(sink + moved)
    return sizes[jax.random.permutation(jax.random.fold_in(stream_key, 2), amount)]


def scatter_about(stream_key, extent, scale, reach, shards=(), held_as=jnp.bfloat16):
    result = jax.random.normal(stream_key, extent, jnp.float32) * scale
    if len(shards) > 0:
        result = level_of(stream_key, extent, shards, -0.22, 0.18) * result
    return jnp.clip(result, min=-reach, max=reach).astype(held_as)


def setup_inputs(seed: int = 0) -> dict:
    splits = jax.random.split(jax.random.key(seed), 16)
    tokens = scatter_about(splits[0], (ROWS, ROW_LEN, D), 1.0, 6.0, ((0, 32),))
    doc_ids = jax.vmap(lambda own: jnp.searchsorted(jnp.cumsum(ragged_sizes(own, DOCS, ROW_LEN, ROW_LEN // 2, 0)), jnp.arange(ROW_LEN), side="right"))(jax.random.split(splits[1], ROWS)).reshape((ROWS, ROW_LEN)).astype(jnp.int32)
    cotangent = scatter_about(splits[2], (ROWS, ROW_LEN, D), 1.0, 6.0, ((0, 32),))
    gain_in = jnp.clip(1.0 + 0.1 * jax.random.normal(splits[3], (D,), jnp.float32), 0.5, 1.5)
    w_query = scatter_about(splits[4], (D, D), D ** -0.5, 0.15625, ((0, 4),), jnp.float32)
    w_key = scatter_about(splits[5], (D, D), D ** -0.5, 0.15625, ((0, 4),), jnp.float32)
    w_value = scatter_about(splits[6], (D, D), D ** -0.5, 0.15625, ((0, 4),), jnp.float32)
    w_house = scatter_about(splits[7], (D, D), D ** -0.5, 0.15625, ((0, 4),), jnp.float32)
    w_rate = scatter_about(splits[8], (D, HEADS), D ** -0.5, 0.15625, ((0, 4),), jnp.float32)
    conv_taps = scatter_about(splits[9], (CONV, D), 0.5, 3.0, ((1, 4),), jnp.float32)
    w_out = scatter_about(splits[10], (D, D), (D // 8) ** -0.5, 0.4375, ((0, 4),), jnp.float32)
    gain_mid = jnp.clip(1.0 + 0.1 * jax.random.normal(splits[11], (D,), jnp.float32), 0.5, 1.5)
    w_gate = scatter_about(splits[12], (D, FF), D ** -0.5, 0.15625, ((0, 4),), jnp.float32)
    w_up = scatter_about(splits[13], (D, FF), D ** -0.5, 0.15625, ((0, 4),), jnp.float32)
    w_down = scatter_about(splits[14], (FF, D), FF ** -0.5, 0.09375, ((0, 4),), jnp.float32)
    return {"tokens": tokens, "doc_ids": doc_ids, "cotangent": cotangent, "gain_in": gain_in, "w_query": w_query, "w_key": w_key, "w_value": w_value, "w_house": w_house, "w_rate": w_rate, "conv_taps": conv_taps, "w_out": w_out, "gain_mid": gain_mid, "w_gate": w_gate, "w_up": w_up, "w_down": w_down}


@jax.custom_vjp
def low(v):
    return lax.optimization_barrier(v.astype(jnp.bfloat16)).astype(jnp.float32)

@jax.custom_vjp
def low_back(v):
    return v

def low_keep(v):
    return (low(v), None)

def low_pass(kept, grad):
    return (grad,)

def back_keep(v):
    return (v, None)

def back_low(kept, grad):
    return (low(grad),)
low.defvjp(low_keep, low_pass)
low_back.defvjp(back_keep, back_low)
epsilon = 1e-06
highest = lax.Precision.HIGHEST

def rms_scale(row_block, gain_row):
    inverse = lax.rsqrt(lax.optimization_barrier(jnp.mean(row_block * row_block, axis=-1, keepdims=True)) + epsilon)
    return row_block * inverse * gain_row

def short_conv(house_raw, tap_values, segment):
    length = house_raw.shape[0]
    summed = house_raw * tap_values[0]
    for offset in range(1, tap_values.shape[0]):
        shifted = jnp.concatenate([jnp.zeros((offset, house_raw.shape[1]), house_raw.dtype), house_raw[:length - offset]], axis=0)
        seg_shift = jnp.concatenate([jnp.full((offset,), -1, jnp.int32), segment[:length - offset].astype(jnp.int32)])
        same_doc = (seg_shift == segment.astype(jnp.int32))[:, None]
        summed = summed + jnp.where(same_doc, shifted * tap_values[offset], 0.0)
    return summed

def unit_rows(mixed_rows, head_count):
    split_rows = mixed_rows.reshape(mixed_rows.shape[:-1] + (head_count, -1))
    inverse = lax.rsqrt(lax.optimization_barrier(jnp.sum(split_rows * split_rows, axis=-1, keepdims=True)) + epsilon)
    return (split_rows * inverse).reshape(mixed_rows.shape)

def outer_dot(left_rows, right_rows):
    return jnp.dot(left_rows, right_rows.T, precision=highest)

def path_head(query_rows, key_rows, value_rows, house_rows, rate_rows, segment):
    length = query_rows.shape[0]
    positions = lax.iota(jnp.int32, length)
    same_doc = segment[:, None] == segment[None, :]
    inclusive = same_doc & (positions[None, :] <= positions[:, None])
    strict = same_doc & (positions[None, :] < positions[:, None])
    lower_part = jnp.where(strict, outer_dot(house_rows, house_rows) * rate_rows[None, :], 0.0)
    right_side = jnp.where(strict, outer_dot(house_rows, key_rows), 0.0)
    system = jnp.eye(length, dtype=query_rows.dtype) + lower_part
    carried = lax.linalg.triangular_solve(system, right_side, left_side=True, lower=True, unit_diagonal=True)
    reach_part = jnp.where(inclusive, outer_dot(query_rows, house_rows), 0.0) * rate_rows[None, :]
    scores = (outer_dot(query_rows, key_rows) - jnp.dot(reach_part, carried, precision=highest)) * query_rows.shape[1] ** (-0.5)
    scores = jnp.where(inclusive, scores, -1e+30)
    row_max = lax.optimization_barrier(jnp.max(scores, axis=1, keepdims=True))
    exp_terms = jnp.where(inclusive, jnp.exp(scores - row_max), 0.0)
    probabilities = exp_terms / lax.optimization_barrier(jnp.sum(exp_terms, axis=1, keepdims=True))
    return jnp.dot(probabilities, value_rows, precision=highest)

def path_attention(query_rows, key_rows, value_rows, house_rows, rate_rows, segment, head_count):
    length, model_width = query_rows.shape

    def by_heads(array):
        return array.reshape(length, head_count, model_width // head_count).transpose(1, 0, 2)

    def per_head(packed):
        return path_head(packed[0], packed[1], packed[2], packed[3], packed[4], segment)
    stacked = lax.map(jax.checkpoint(per_head), (by_heads(query_rows), by_heads(key_rows), by_heads(value_rows), by_heads(house_rows), rate_rows.T))
    return stacked.transpose(1, 0, 2).reshape(length, model_width)

def project(left_rows, matrix):
    return jnp.dot(left_rows, matrix, precision=highest)

def forward(inputs, doc_ids, gain_in, w_query, w_key, w_value, w_house, w_rate, conv_taps, w_out, gain_mid, w_gate, w_up, w_down):
    row_count, length, model_width = inputs.shape
    head_count = w_rate.shape[1]
    flat_rows = inputs.reshape(row_count * length, model_width)
    normed = low(rms_scale(flat_rows, low(gain_in)))
    query_rows = low_back(low(project(normed, low(w_query))))
    key_rows = low_back(low(project(normed, low(w_key))))
    value_rows = low_back(low(project(normed, low(w_value))))
    house_raw = low_back(project(normed, low(w_house))).reshape(row_count, length, model_width)
    rate_rows = 2.0 * jax.nn.sigmoid(low_back(project(normed, low(w_rate))))
    conv_all = jax.vmap(short_conv, in_axes=(0, None, 0))(house_raw, low(conv_taps), doc_ids)
    house_rows = low(unit_rows(conv_all, head_count))

    def attend_row(packed):
        return path_attention(packed[0], packed[1], packed[2], packed[3], packed[4], packed[5], head_count)
    attended = lax.map(jax.checkpoint(attend_row), (query_rows.reshape(row_count, length, model_width), key_rows.reshape(row_count, length, model_width), value_rows.reshape(row_count, length, model_width), house_rows, rate_rows.reshape(row_count, length, head_count), doc_ids))
    branch = low_back(project(low(attended.reshape(row_count * length, model_width)), low(w_out)))
    middle = flat_rows + branch
    normed_mid = low(rms_scale(middle, low(gain_mid)))
    gate_rows = low_back(project(normed_mid, low(w_gate)))
    up_rows = low_back(project(normed_mid, low(w_up)))
    hidden = low(jax.nn.silu(gate_rows) * up_rows)
    outputs = middle + project(hidden, low(w_down))
    return outputs.reshape(row_count, length, model_width)

def reference(tokens, doc_ids, cotangent, gain_in, w_query, w_key, w_value, w_house, w_rate, conv_taps, w_out, gain_mid, w_gate, w_up, w_down):

    def run(inputs, g_in, m_query, m_key, m_value, m_house, m_rate, m_taps, m_out, g_mid, m_gate, m_up, m_down):
        return forward(inputs, doc_ids, g_in, m_query, m_key, m_value, m_house, m_rate, m_taps, m_out, g_mid, m_gate, m_up, m_down)
    outputs, backward = jax.vjp(run, tokens.astype(jnp.float32), gain_in, w_query, w_key, w_value, w_house, w_rate, conv_taps, w_out, gain_mid, w_gate, w_up, w_down)
    grads = backward(cotangent.astype(jnp.float32))
    return (outputs.astype(jnp.bfloat16), grads[0], grads[1], grads[2], grads[3], grads[4], grads[5], grads[6], grads[7], grads[8], grads[9], grads[10], grads[11], grads[12])
```

```python
import functools
import jax
import jax.numpy as jnp
from jax import lax
from jax.experimental import pallas as pl
from jax.experimental.pallas import tpu as pltpu
from jax.sharding import PartitionSpec as P

EPS = 1e-06
HALF = jnp.bfloat16
SINGLE = jnp.float32


def mm(left, right):
    return lax.dot_general(left, right, (((1,), (0,)), ((), ())), preferred_element_type=SINGLE)


def mm_nt(left, right):
    return lax.dot_general(left, right, (((1,), (1,)), ((), ())), preferred_element_type=SINGLE)


def mm_tn(left, right):
    return lax.dot_general(left, right, (((0,), (0,)), ((), ())), preferred_element_type=SINGLE)


def conv_parts(raw, taps, marks, taps_count):
    shifted = [raw]
    total = raw * taps[0:1, :]
    for k in range(1, taps_count):
        moved = pltpu.roll(raw, k, 0) * marks[:, k : k + 1]
        shifted.append(moved)
        total = total + moved * taps[k : k + 1, :]
    return shifted, total


def attn_forward_kernel(
    span, dim, count, taps_count,
    q_ref, k_ref, v_ref, raw_ref, rate_ref, taps_ref, marks_ref, segc_ref, segr_ref,
    out_ref, w_ref, t_ref, c_ref, p_ref,
):
    blocks = q_ref.shape[0] // span
    marks = marks_ref[...]
    row_id = lax.broadcasted_iota(jnp.int32, (span, span), 0)
    col_id = lax.broadcasted_iota(jnp.int32, (span, span), 1)
    eye = jnp.where(row_id == col_id, 1.0, 0.0)
    sizes = []
    size = 1
    while size < span:
        sizes.append(size)
        size *= 2
    level_of = {}
    for size in sizes:
        level_of[size] = ((row_id // (2 * size)) == (col_id // (2 * size))) & (
            (row_id // size) > (col_id // size)
        )
    strict = []
    inclusive = []
    for u in range(blocks):
        rows = slice(u * span, (u + 1) * span)
        same = segc_ref[rows, 0:1] == segr_ref[0:1, rows]
        strict.append(same & (col_id < row_id))
        inclusive.append(same & (col_id <= row_id))
    for h in range(count):
        cols = slice(h * dim, (h + 1) * dim)
        shifted, mixed = conv_parts(raw_ref[:, cols], taps_ref[:, cols], marks, taps_count)
        inverse = lax.rsqrt(jnp.sum(mixed * mixed, axis=-1, keepdims=True) + EPS)
        w_ref[:, cols] = (mixed * inverse).astype(HALF)
    units = [(h, u) for h in range(count) for u in range(blocks)]
    rates = {}
    lower = {}
    inv = {}
    for h, u in units:
        rows = slice(u * span, (u + 1) * span)
        cols = slice(h * dim, (h + 1) * dim)
        w = w_ref[rows, cols]
        rates[h, u] = rate_ref[0, h : h + 1, rows]
        lw = jnp.where(strict[u], mm_nt(w, w) * rates[h, u], 0.0)
        lower[h, u] = lw.astype(HALF)
        inv[h, u] = eye - jnp.where(level_of[1], lw, 0.0)
    for size in sizes[1:]:
        half_inv = {}
        inner = {}
        for unit in units:
            half_inv[unit] = inv[unit].astype(HALF)
            inner[unit] = mm(jnp.where(level_of[size], lower[unit], jnp.zeros_like(lower[unit])), half_inv[unit])
        for unit in units:
            inv[unit] = inv[unit] - mm(half_inv[unit], inner[unit].astype(HALF))
    for h, u in units:
        rows = slice(u * span, (u + 1) * span)
        cols = slice(h * dim, (h + 1) * dim)
        w = w_ref[rows, cols]
        q = q_ref[rows, cols]
        k = k_ref[rows, cols]
        tri = inv[h, u].astype(HALF)
        t_ref[h * blocks + u] = tri
        right = jnp.where(strict[u], mm_nt(w, k), 0.0).astype(HALF)
        carried = mm(tri, right).astype(HALF)
        c_ref[h * blocks + u] = carried
        reach = (jnp.where(inclusive[u], mm_nt(q, w), 0.0) * rates[h, u]).astype(HALF)
        scores = (mm_nt(q, k) - mm(reach, carried)) * dim ** (-0.5)
        scores = jnp.where(inclusive[u], scores, -1e30)
        terms = jnp.exp(scores - jnp.max(scores, axis=1, keepdims=True))
        probs = (terms / jnp.sum(terms, axis=1, keepdims=True)).astype(HALF)
        p_ref[h * blocks + u] = probs
        out_ref[rows, cols] = mm(probs, v_ref[rows, cols]).astype(HALF)


def attn_backward_kernel(
    span, dim, count, taps_count,
    q_ref, k_ref, v_ref, w_ref, raw_ref, rate_ref, taps_ref, marks_ref, segc_ref, segr_ref,
    grad_ref, t_ref, c_ref, p_ref,
    dq_ref, dk_ref, dv_ref, draw_ref, drate_ref, dtaps_ref, dw_ref,
):
    blocks = q_ref.shape[0] // span
    marks = marks_ref[...]
    row_id = lax.broadcasted_iota(jnp.int32, (span, span), 0)
    col_id = lax.broadcasted_iota(jnp.int32, (span, span), 1)
    scale = dim ** (-0.5)
    for u in range(blocks):
        rows = slice(u * span, (u + 1) * span)
        same = segc_ref[rows, 0:1] == segr_ref[0:1, rows]
        strict = same & (col_id < row_id)
        inclusive = same & (col_id <= row_id)
        for h in range(count):
            cols = slice(h * dim, (h + 1) * dim)
            unit = h * blocks + u
            q = q_ref[rows, cols]
            k = k_ref[rows, cols]
            v = v_ref[rows, cols]
            w = w_ref[rows, cols]
            grad = grad_ref[rows, cols]
            rate = rate_ref[0, h : h + 1, rows]
            probs = p_ref[unit]
            carried = c_ref[unit]
            tri = t_ref[unit]
            dprobs = mm_nt(grad, v)
            dv_ref[rows, cols] = mm_tn(probs, grad).astype(HALF)
            probs = probs.astype(SINGLE)
            weighted = probs * dprobs
            dscore = ((weighted - probs * jnp.sum(weighted, axis=1, keepdims=True)) * scale).astype(HALF)
            reach_raw = jnp.where(inclusive, mm_nt(q, w), 0.0)
            reach = (reach_raw * rate).astype(HALF)
            dreach = -mm_nt(dscore, carried)
            drate = jnp.sum(dreach * reach_raw, axis=0, keepdims=True)
            dreach = (jnp.where(inclusive, dreach, 0.0) * rate).astype(HALF)
            dcarried = (-mm_tn(reach, dscore)).astype(HALF)
            dright = jnp.where(strict, mm_tn(tri, dcarried), 0.0).astype(HALF)
            dlower = jnp.where(strict, -mm_nt(dright, carried), 0.0)
            drate = drate + jnp.sum(dlower * mm_nt(w, w), axis=0, keepdims=True)
            dlower = (dlower * rate).astype(HALF)
            dq_ref[rows, cols] = (mm(dscore, k) + mm(dreach, w)).astype(HALF)
            dk_ref[rows, cols] = (mm_tn(dscore, q) + mm_tn(dright, w)).astype(HALF)
            dw_ref[rows, cols] = mm_tn(dreach, q) + mm(dright, k) + mm(dlower, w) + mm_tn(dlower, w)
            drate_ref[0, h : h + 1, rows] = drate
    length = q_ref.shape[0]
    for h in range(count):
        cols = slice(h * dim, (h + 1) * dim)
        taps = taps_ref[:, cols]
        shifted, mixed = conv_parts(raw_ref[:, cols], taps, marks, taps_count)
        inverse = lax.rsqrt(jnp.sum(mixed * mixed, axis=-1, keepdims=True) + EPS)
        unit_rows = mixed * inverse
        dw = dw_ref[:, cols]
        dmixed = inverse * (dw - unit_rows * jnp.sum(dw * unit_rows, axis=-1, keepdims=True))
        draw = dmixed * taps[0:1, :]
        dtaps = [jnp.sum(dmixed * shifted[0], axis=0, keepdims=True)]
        for k in range(1, taps_count):
            dtaps.append(jnp.sum(dmixed * shifted[k], axis=0, keepdims=True))
            draw = draw + pltpu.roll(dmixed * marks[:, k : k + 1], length - k, 0) * taps[k : k + 1, :]
        draw_ref[:, cols] = draw.astype(HALF)
        dtaps_ref[:, cols] = jnp.concatenate(dtaps, axis=0)


def attn_forward(q, k, v, raw, rate, taps, marks, segc, segr, dim, count, span):
    length, width = q.shape
    groups = width // (dim * count)
    units = count * (length // span)
    wide = pl.BlockSpec((length, count * dim), lambda g: (0, g))
    whole = lambda a: pl.BlockSpec(a.shape, lambda g: (0,) * a.ndim)
    square = pl.BlockSpec((units, span, span), lambda g: (g, 0, 0))
    square_shape = jax.ShapeDtypeStruct((units * groups, span, span), HALF)
    return pl.pallas_call(
        functools.partial(attn_forward_kernel, span, dim, count, taps.shape[0]),
        grid=(groups,),
        in_specs=[
            wide, wide, wide, wide,
            pl.BlockSpec((1, count, length), lambda g: (g, 0, 0)),
            pl.BlockSpec((taps.shape[0], count * dim), lambda g: (0, g)),
            whole(marks), whole(segc), whole(segr),
        ],
        out_specs=[wide, wide, square, square, square],
        out_shape=[
            jax.ShapeDtypeStruct((length, width), HALF),
            jax.ShapeDtypeStruct((length, width), HALF),
            square_shape, square_shape, square_shape,
        ],
        compiler_params=pltpu.CompilerParams(vmem_limit_bytes=56 * 1024 * 1024),
        name="attend",
    )(q, k, v, raw, rate, taps, marks, segc, segr)


def attn_backward(q, k, v, w, raw, rate, taps, marks, segc, segr, grad, tri, carried, probs, dim, count, span):
    length, width = q.shape
    groups = width // (dim * count)
    units = count * (length // span)
    wide = pl.BlockSpec((length, count * dim), lambda g: (0, g))
    whole = lambda a: pl.BlockSpec(a.shape, lambda g: (0,) * a.ndim)
    square = pl.BlockSpec((units, span, span), lambda g: (g, 0, 0))
    rates = pl.BlockSpec((1, count, length), lambda g: (g, 0, 0))
    tap_spec = pl.BlockSpec((taps.shape[0], count * dim), lambda g: (0, g))
    wide_shape = jax.ShapeDtypeStruct((length, width), HALF)
    return pl.pallas_call(
        functools.partial(attn_backward_kernel, span, dim, count, taps.shape[0]),
        grid=(groups,),
        in_specs=[
            wide, wide, wide, wide, wide, rates, tap_spec,
            whole(marks), whole(segc), whole(segr), wide, square, square, square,
        ],
        out_specs=[wide, wide, wide, wide, rates, tap_spec],
        out_shape=[
            wide_shape, wide_shape, wide_shape, wide_shape,
            jax.ShapeDtypeStruct(rate.shape, SINGLE),
            jax.ShapeDtypeStruct(taps.shape, SINGLE),
        ],
        scratch_shapes=[pltpu.VMEM((length, count * dim), SINGLE)],
        compiler_params=pltpu.CompilerParams(vmem_limit_bytes=56 * 1024 * 1024),
        name="attend_back",
    )(q, k, v, w, raw, rate, taps, marks, segc, segr, grad, tri, carried, probs)

epsilon = 1e-06
highest = lax.Precision.HIGHEST


def rms_scale(row_block, gain_row):
    inverse = lax.rsqrt(jnp.mean(row_block * row_block, axis=-1, keepdims=True) + epsilon)
    return row_block * inverse * gain_row


def dot_plain(left_rows, right_rows):
    return jnp.dot(left_rows, right_rows, preferred_element_type=jnp.float32)


def dot_left_t(left_rows, right_rows):
    return lax.dot_general(
        left_rows, right_rows, (((0,), (0,)), ((), ())), preferred_element_type=jnp.float32
    )


def dot_right_t(left_rows, right_rows):
    return lax.dot_general(
        left_rows, right_rows, (((1,), (1,)), ((), ())), preferred_element_type=jnp.float32
    )


def fetch_attention(gain_in, w_query, w_key, w_value, w_house, w_rate, conv_taps, w_out):
    half = jnp.bfloat16
    return (
        lax.all_gather(gain_in.astype(half), "fsdp", axis=0, tiled=True),
        lax.all_gather(w_query.astype(half), "fsdp", axis=0, tiled=True),
        lax.all_gather(w_key.astype(half), "fsdp", axis=0, tiled=True),
        lax.all_gather(w_value.astype(half), "fsdp", axis=0, tiled=True),
        lax.all_gather(w_house.astype(half), "fsdp", axis=0, tiled=True),
        lax.all_gather(w_rate.astype(half), "fsdp", axis=0, tiled=True),
        lax.all_gather(conv_taps.astype(half), "fsdp", axis=1, tiled=True),
        lax.all_gather(w_out.astype(half), "fsdp", axis=0, tiled=True),
    )


def fetch_feed(gain_mid, w_gate, w_up, w_down):
    half = jnp.bfloat16
    return (
        lax.all_gather(gain_mid.astype(half), "fsdp", axis=0, tiled=True),
        lax.all_gather(w_gate.astype(half), "fsdp", axis=0, tiled=True),
        lax.all_gather(w_up.astype(half), "fsdp", axis=0, tiled=True),
        lax.all_gather(w_down.astype(half), "fsdp", axis=0, tiled=True),
    )


def local(
    tokens,
    doc_ids,
    cotangent,
    gain_in,
    w_query,
    w_key,
    w_value,
    w_house,
    w_rate,
    conv_taps,
    w_out,
    gain_mid,
    w_gate,
    w_up,
    w_down,
):
    half = jnp.bfloat16
    single = jnp.float32
    head_count = w_rate.shape[1]
    length = tokens.shape[1]
    span = length // 2
    dim = tokens.shape[2] // head_count
    doc_row = doc_ids[0]
    start = jnp.argmax(doc_row[: length - span + 1] == doc_row[span - 1 :])
    position = lax.iota(jnp.int32, length)
    source = (position + start) % length
    turn = (source[:, None] == position[None, :]).astype(half)
    segment = jnp.sum(jnp.where(turn > 0, doc_row[None, :], 0), axis=1)
    flat_rows = dot_plain(turn, tokens[0])
    upstream = dot_plain(turn, cotangent[0]).astype(half)
    marks = jnp.stack(
        [
            ((jnp.roll(segment, k) == segment) & (position >= k)).astype(single)
            for k in range(conv_taps.shape[0])
        ],
        axis=1,
    )
    count = 3
    attn_set = fetch_attention(gain_in, w_query, w_key, w_value, w_house, w_rate, conv_taps, w_out)
    feed_set = fetch_feed(gain_mid, w_gate, w_up, w_down)
    gain_one, mat_query, mat_key, mat_value, mat_house, mat_rate, tap_half, mat_out = attn_set
    gain_two, mat_gate, mat_up, mat_down = feed_set
    gain_first = gain_one.astype(single)
    normed = rms_scale(flat_rows, gain_first).astype(half)
    query_rows = dot_plain(normed, mat_query).astype(half)
    key_rows = dot_plain(normed, mat_key).astype(half)
    value_rows = dot_plain(normed, mat_value).astype(half)
    house_raw = dot_plain(normed, mat_house)
    rate_sig = jax.nn.sigmoid(
        lax.dot_general(mat_rate, normed, (((0,), (1,)), ((), ())), preferred_element_type=single)
    )
    rate_rows = (2.0 * rate_sig).reshape(head_count // count, count, length)
    tap_values = tap_half.astype(single)
    attended, house_rows, tri, carried, probs = attn_forward(
        query_rows, key_rows, value_rows, house_raw, rate_rows, tap_values, marks,
        segment[:, None], segment[None, :], dim, count, span,
    )
    middle = flat_rows + dot_plain(attended, mat_out)
    gain_second = gain_two.astype(single)
    normed_mid = rms_scale(middle, gain_second).astype(half)
    gate_rows = dot_plain(normed_mid, mat_gate)
    up_rows = dot_plain(normed_mid, mat_up)
    gate_sig = jax.nn.sigmoid(gate_rows)
    hidden = (gate_rows * gate_sig * up_rows).astype(half)
    result = (middle + dot_plain(hidden, mat_down)).astype(half)
    attn_set = fetch_attention(gain_in, w_query, w_key, w_value, w_house, w_rate, conv_taps, w_out)
    feed_set = fetch_feed(gain_mid, w_gate, w_up, w_down)
    gain_one, mat_query, mat_key, mat_value, mat_house, mat_rate, tap_half, mat_out = attn_set
    gain_two, mat_gate, mat_up, mat_down = feed_set
    grad_down = dot_left_t(hidden, upstream)
    grad_hidden = dot_right_t(upstream, mat_down)
    grad_up_rows = (grad_hidden * gate_rows * gate_sig).astype(half)
    grad_gate_rows = (
        grad_hidden * up_rows * gate_sig * (1.0 + gate_rows * (1.0 - gate_sig))
    ).astype(half)
    grad_gate = dot_left_t(normed_mid, grad_gate_rows)
    grad_up = dot_left_t(normed_mid, grad_up_rows)
    grad_normed_mid = dot_right_t(grad_gate_rows, mat_gate) + dot_right_t(grad_up_rows, mat_up)
    unused_mid, mid_back = jax.vjp(rms_scale, middle, gain_second)
    grad_mid_norm, grad_gain_mid = mid_back(grad_normed_mid)
    feed_grads = (
        lax.psum_scatter(
            grad_gain_mid.astype(jnp.bfloat16), "fsdp", scatter_dimension=0, tiled=True
        ).astype(jnp.float32),
        lax.psum_scatter(
            grad_gate.astype(jnp.bfloat16), "fsdp", scatter_dimension=0, tiled=True
        ).astype(jnp.float32),
        lax.psum_scatter(
            grad_up.astype(jnp.bfloat16), "fsdp", scatter_dimension=0, tiled=True
        ).astype(jnp.float32),
        lax.psum_scatter(
            grad_down.astype(jnp.bfloat16), "fsdp", scatter_dimension=0, tiled=True
        ).astype(jnp.float32),
    )
    grad_middle = upstream.astype(single) + grad_mid_norm
    grad_branch = grad_middle.astype(half)
    grad_wout = dot_left_t(attended, grad_branch)
    grad_attended = dot_right_t(grad_branch, mat_out)
    (grad_query_rows, grad_key_rows, grad_value_rows, grad_house_rows, grad_rate_f, grad_taps) = attn_backward(
        query_rows, key_rows, value_rows, house_rows, house_raw, rate_rows, tap_values, marks,
        segment[:, None], segment[None, :], grad_attended.astype(half), tri, carried, probs, dim, count, span,
    )
    grad_rate_f = grad_rate_f.reshape(head_count, length)
    grad_rate_rows = (grad_rate_f * 2.0 * rate_sig * (1.0 - rate_sig)).astype(half).T
    grad_wquery = dot_left_t(normed, grad_query_rows)
    grad_wkey = dot_left_t(normed, grad_key_rows)
    grad_wvalue = dot_left_t(normed, grad_value_rows)
    grad_whouse = dot_left_t(normed, grad_house_rows)
    grad_wrate = dot_left_t(normed, grad_rate_rows)
    grad_normed = (
        dot_right_t(grad_query_rows, mat_query)
        + dot_right_t(grad_key_rows, mat_key)
        + dot_right_t(grad_value_rows, mat_value)
        + dot_right_t(grad_house_rows, mat_house)
        + dot_right_t(grad_rate_rows, mat_rate)
    )
    unused_in, in_back = jax.vjp(rms_scale, flat_rows, gain_first)
    grad_flat_norm, grad_gain_in = in_back(grad_normed)
    grad_tokens = grad_middle + grad_flat_norm
    attn_grads = (
        lax.psum_scatter(
            grad_gain_in.astype(jnp.bfloat16), "fsdp", scatter_dimension=0, tiled=True
        ).astype(jnp.float32),
        lax.psum_scatter(
            grad_wquery.astype(jnp.bfloat16), "fsdp", scatter_dimension=0, tiled=True
        ).astype(jnp.float32),
        lax.psum_scatter(
            grad_wkey.astype(jnp.bfloat16), "fsdp", scatter_dimension=0, tiled=True
        ).astype(jnp.float32),
        lax.psum_scatter(
            grad_wvalue.astype(jnp.bfloat16), "fsdp", scatter_dimension=0, tiled=True
        ).astype(jnp.float32),
        lax.psum_scatter(
            grad_whouse.astype(jnp.bfloat16), "fsdp", scatter_dimension=0, tiled=True
        ).astype(jnp.float32),
        lax.psum_scatter(
            grad_wrate.astype(jnp.bfloat16), "fsdp", scatter_dimension=0, tiled=True
        ).astype(jnp.float32),
        lax.psum_scatter(
            grad_taps.astype(jnp.bfloat16), "fsdp", scatter_dimension=1, tiled=True
        ).astype(jnp.float32),
        lax.psum_scatter(
            grad_wout.astype(jnp.bfloat16), "fsdp", scatter_dimension=0, tiled=True
        ).astype(jnp.float32),
    )
    summed = (
        lax.psum(attn_grads[0].astype(jnp.bfloat16), "grp").astype(jnp.float32),
        lax.psum(attn_grads[1].astype(jnp.bfloat16), "grp").astype(jnp.float32),
        lax.psum(attn_grads[2].astype(jnp.bfloat16), "grp").astype(jnp.float32),
        lax.psum(attn_grads[3].astype(jnp.bfloat16), "grp").astype(jnp.float32),
        lax.psum(attn_grads[4].astype(jnp.bfloat16), "grp").astype(jnp.float32),
        lax.psum(attn_grads[5].astype(jnp.bfloat16), "grp").astype(jnp.float32),
        lax.psum(attn_grads[6].astype(jnp.bfloat16), "grp").astype(jnp.float32),
        lax.psum(attn_grads[7].astype(jnp.bfloat16), "grp").astype(jnp.float32),
        lax.psum(feed_grads[0].astype(jnp.bfloat16), "grp").astype(jnp.float32),
        lax.psum(feed_grads[1].astype(jnp.bfloat16), "grp").astype(jnp.float32),
        lax.psum(feed_grads[2].astype(jnp.bfloat16), "grp").astype(jnp.float32),
        lax.psum(feed_grads[3].astype(jnp.bfloat16), "grp").astype(jnp.float32),
    )
    result = dot_left_t(turn, result).astype(half)
    high = grad_tokens.astype(half)
    low = (grad_tokens - high.astype(single)).astype(half)
    grad_tokens = dot_left_t(turn, high) + dot_left_t(turn, low)
    return (
        result[None],
        grad_tokens[None],
        summed[0],
        summed[1],
        summed[2],
        summed[3],
        summed[4],
        summed[5],
        summed[6],
        summed[7],
        summed[8],
        summed[9],
        summed[10],
        summed[11],
    )


def solution(mesh):
    return jax.shard_map(
        local,
        mesh=mesh,
        in_specs=(
            P(("grp", "fsdp"), None, None),
            P(("grp", "fsdp"), None),
            P(("grp", "fsdp"), None, None),
            P("fsdp"),
            P("fsdp", None),
            P("fsdp", None),
            P("fsdp", None),
            P("fsdp", None),
            P("fsdp", None),
            P(None, "fsdp"),
            P("fsdp", None),
            P("fsdp"),
            P("fsdp", None),
            P("fsdp", None),
            P("fsdp", None),
        ),
        out_specs=(
            P(("grp", "fsdp"), None, None),
            P(("grp", "fsdp"), None, None),
            P("fsdp"),
            P("fsdp", None),
            P("fsdp", None),
            P("fsdp", None),
            P("fsdp", None),
            P("fsdp", None),
            P(None, "fsdp"),
            P("fsdp", None),
            P("fsdp"),
            P("fsdp", None),
            P("fsdp", None),
            P("fsdp", None),
        ),
        check_vma=False,
    )
```

```python
import functools
import jax
import jax.numpy as jnp
from jax import lax
from jax.experimental import pallas as pl
from jax.experimental.pallas import tpu as pltpu
from jax.sharding import PartitionSpec as P

EPS = 1e-06
HALF = jnp.bfloat16
SINGLE = jnp.float32


def mm(left, right):
    return lax.dot_general(left, right, (((1,), (0,)), ((), ())), preferred_element_type=SINGLE)


def mm_nt(left, right):
    return lax.dot_general(left, right, (((1,), (1,)), ((), ())), preferred_element_type=SINGLE)


def mm_tn(left, right):
    return lax.dot_general(left, right, (((0,), (0,)), ((), ())), preferred_element_type=SINGLE)


def conv_parts(raw, taps, marks, taps_count):
    shifted = [raw]
    total = raw * taps[0:1, :]
    for k in range(1, taps_count):
        moved = pltpu.roll(raw, k, 0) * marks[:, k : k + 1]
        shifted.append(moved)
        total = total + moved * taps[k : k + 1, :]
    return shifted, total


def attn_forward_kernel(
    span, dim, count, taps_count, number, *refs
):
    normed_ref = refs[0]
    piece_refs = refs[1 : 1 + number]
    rate_ref, taps_ref, marks_ref, segc_ref, segr_ref = refs[1 + number : 6 + number]
    out_ref, qkv_ref, raw_ref, w_ref, t_ref, c_ref, p_ref = refs[6 + number :]
    blocks = normed_ref.shape[0] // span
    wide = count * dim
    depth = normed_ref.shape[1] // number
    for m in (3, 0, 1, 2):
        total = mm(normed_ref[:, :depth], piece_refs[0][:, m * wide : (m + 1) * wide])
        for r in range(1, number):
            total = total + mm(
                normed_ref[:, r * depth : (r + 1) * depth], piece_refs[r][:, m * wide : (m + 1) * wide]
            )
        if m == 3:
            raw_ref[...] = total
        else:
            qkv_ref[:, m * wide : (m + 1) * wide] = total.astype(HALF)
    q_ref, k_ref, v_ref = [qkv_ref.at[:, m * wide : (m + 1) * wide] for m in range(3)]
    marks = marks_ref[...]
    row_id = lax.broadcasted_iota(jnp.int32, (span, span), 0)
    col_id = lax.broadcasted_iota(jnp.int32, (span, span), 1)
    eye = jnp.where(row_id == col_id, 1.0, 0.0)
    sizes = []
    size = 1
    while size < span:
        sizes.append(size)
        size *= 2
    level_of = {}
    for size in sizes:
        level_of[size] = ((row_id // (2 * size)) == (col_id // (2 * size))) & (
            (row_id // size) > (col_id // size)
        )
    strict = []
    inclusive = []
    for u in range(blocks):
        rows = slice(u * span, (u + 1) * span)
        same = segc_ref[rows, 0:1] == segr_ref[0:1, rows]
        strict.append(same & (col_id < row_id))
        inclusive.append(same & (col_id <= row_id))
    for h in range(count):
        cols = slice(h * dim, (h + 1) * dim)
        shifted, mixed = conv_parts(raw_ref[:, cols], taps_ref[:, cols], marks, taps_count)
        inverse = lax.rsqrt(jnp.sum(mixed * mixed, axis=-1, keepdims=True) + EPS)
        w_ref[:, cols] = (mixed * inverse).astype(HALF)
    units = [(h, u) for h in range(count) for u in range(blocks)]
    rates = {}
    lower = {}
    inv = {}
    for h, u in units:
        rows = slice(u * span, (u + 1) * span)
        cols = slice(h * dim, (h + 1) * dim)
        w = w_ref[rows, cols]
        rates[h, u] = rate_ref[h : h + 1, rows]
        lw = jnp.where(strict[u], mm_nt(w, w) * rates[h, u], 0.0)
        lower[h, u] = lw.astype(HALF)
        inv[h, u] = eye - jnp.where(level_of[1], lw, 0.0)
    for size in sizes[1:]:
        half_inv = {}
        inner = {}
        for unit in units:
            half_inv[unit] = inv[unit].astype(HALF)
            inner[unit] = mm(jnp.where(level_of[size], lower[unit], jnp.zeros_like(lower[unit])), half_inv[unit])
        for unit in units:
            inv[unit] = inv[unit] - mm(half_inv[unit], inner[unit].astype(HALF))
    for h, u in units:
        rows = slice(u * span, (u + 1) * span)
        cols = slice(h * dim, (h + 1) * dim)
        w = w_ref[rows, cols]
        q = q_ref[rows, cols]
        k = k_ref[rows, cols]
        tri = inv[h, u].astype(HALF)
        t_ref[h * blocks + u] = tri
        right = jnp.where(strict[u], mm_nt(w, k), 0.0).astype(HALF)
        carried = mm(tri, right).astype(HALF)
        c_ref[h * blocks + u] = carried
        reach = (jnp.where(inclusive[u], mm_nt(q, w), 0.0) * rates[h, u]).astype(HALF)
        scores = (mm_nt(q, k) - mm(reach, carried)) * dim ** (-0.5)
        scores = jnp.where(inclusive[u], scores, -1e30)
        terms = jnp.exp(scores - jnp.max(scores, axis=1, keepdims=True))
        probs = (terms / jnp.sum(terms, axis=1, keepdims=True)).astype(HALF)
        p_ref[h * blocks + u] = probs
        out_ref[rows, cols] = mm(probs, v_ref[rows, cols]).astype(HALF)


def attn_backward_kernel(
    span, dim, count, taps_count,
    qkv_ref, w_ref, raw_ref, rate_ref, taps_ref, marks_ref, segc_ref, segr_ref, grad_ref, t_ref, c_ref, p_ref,
    out_ref, drate_ref, dtaps_ref, dw_ref,
):
    blocks = qkv_ref.shape[0] // span
    wide = count * dim
    q_ref, k_ref, v_ref = [qkv_ref.at[:, m * wide : (m + 1) * wide] for m in range(3)]
    dq_ref, dk_ref, dv_ref, draw_ref = [out_ref.at[:, m * wide : (m + 1) * wide] for m in range(4)]
    marks = marks_ref[...]
    row_id = lax.broadcasted_iota(jnp.int32, (span, span), 0)
    col_id = lax.broadcasted_iota(jnp.int32, (span, span), 1)
    scale = dim ** (-0.5)
    for u in range(blocks):
        rows = slice(u * span, (u + 1) * span)
        same = segc_ref[rows, 0:1] == segr_ref[0:1, rows]
        strict = same & (col_id < row_id)
        inclusive = same & (col_id <= row_id)
        for h in range(count):
            cols = slice(h * dim, (h + 1) * dim)
            unit = h * blocks + u
            q = q_ref[rows, cols]
            k = k_ref[rows, cols]
            v = v_ref[rows, cols]
            w = w_ref[rows, cols]
            grad = grad_ref[0, rows, cols]
            rate = rate_ref[h : h + 1, rows]
            probs = p_ref[unit]
            carried = c_ref[unit]
            tri = t_ref[unit]
            dprobs = mm_nt(grad, v)
            dv_ref[rows, cols] = mm_tn(probs, grad).astype(HALF)
            probs = probs.astype(SINGLE)
            weighted = probs * dprobs
            dscore = ((weighted - probs * jnp.sum(weighted, axis=1, keepdims=True)) * scale).astype(HALF)
            reach_raw = jnp.where(inclusive, mm_nt(q, w), 0.0)
            reach = (reach_raw * rate).astype(HALF)
            dreach = -mm_nt(dscore, carried)
            drate = jnp.sum(dreach * reach_raw, axis=0, keepdims=True)
            dreach = (jnp.where(inclusive, dreach, 0.0) * rate).astype(HALF)
            dcarried = (-mm_tn(reach, dscore)).astype(HALF)
            dright = jnp.where(strict, mm_tn(tri, dcarried), 0.0).astype(HALF)
            dlower = jnp.where(strict, -mm_nt(dright, carried), 0.0)
            drate = drate + jnp.sum(dlower * mm_nt(w, w), axis=0, keepdims=True)
            dlower = (dlower * rate).astype(HALF)
            dq_ref[rows, cols] = (mm(dscore, k) + mm(dreach, w)).astype(HALF)
            dk_ref[rows, cols] = (mm_tn(dscore, q) + mm_tn(dright, w)).astype(HALF)
            dw_ref[rows, cols] = mm_tn(dreach, q) + mm(dright, k) + mm(dlower, w) + mm_tn(dlower, w)
            drate_ref[h : h + 1, rows] = drate
    length = q_ref.shape[0]
    for h in range(count):
        cols = slice(h * dim, (h + 1) * dim)
        taps = taps_ref[:, cols]
        shifted, mixed = conv_parts(raw_ref[:, cols], taps, marks, taps_count)
        inverse = lax.rsqrt(jnp.sum(mixed * mixed, axis=-1, keepdims=True) + EPS)
        unit_rows = mixed * inverse
        dw = dw_ref[:, cols]
        dmixed = inverse * (dw - unit_rows * jnp.sum(dw * unit_rows, axis=-1, keepdims=True))
        draw = dmixed * taps[0:1, :]
        dtaps = [jnp.sum(dmixed * shifted[0], axis=0, keepdims=True)]
        for k in range(1, taps_count):
            dtaps.append(jnp.sum(dmixed * shifted[k], axis=0, keepdims=True))
            draw = draw + pltpu.roll(dmixed * marks[:, k : k + 1], length - k, 0) * taps[k : k + 1, :]
        draw_ref[:, cols] = draw.astype(HALF)
        dtaps_ref[:, cols] = jnp.concatenate(dtaps, axis=0)


def attn_forward(normed, pieces, rate, taps, marks, segc, segr, dim, span):
    length = normed.shape[0]
    count = rate.shape[0]
    wide = count * dim
    units = count * (length // span)
    square = jax.ShapeDtypeStruct((units, span, span), HALF)
    return pl.pallas_call(
        functools.partial(attn_forward_kernel, span, dim, count, taps.shape[0], len(pieces)),
        out_shape=[
            jax.ShapeDtypeStruct((length, wide), HALF),
            jax.ShapeDtypeStruct((length, 3 * wide), HALF),
            jax.ShapeDtypeStruct((length, wide), SINGLE),
            jax.ShapeDtypeStruct((length, wide), HALF),
            square, square, square,
        ],
        compiler_params=pltpu.CompilerParams(vmem_limit_bytes=48 * 1024 * 1024),
        cost_estimate=pl.CostEstimate(flops=16000000000, bytes_accessed=12000000, transcendentals=0),
        name="attend",
    )(normed, *pieces, rate, taps, marks, segc, segr)


def attn_backward(qkv, w, raw, rate, taps, marks, segc, segr, grads, group, tri, carried, probs, dim, span):
    length = qkv.shape[0]
    count = rate.shape[0]
    wide = count * dim
    whole = lambda a: pl.BlockSpec(a.shape, lambda g: (0,) * a.ndim)
    small = lambda shape: pl.BlockSpec(shape, lambda g: (0, 0))
    return pl.pallas_call(
        functools.partial(attn_backward_kernel, span, dim, count, taps.shape[0]),
        grid=(1,),
        in_specs=[whole(a) for a in (qkv, w, raw, rate, taps, marks, segc, segr)]
        + [pl.BlockSpec((1, length, wide), lambda g: (group, 0, 0))]
        + [whole(a) for a in (tri, carried, probs)],
        out_specs=[small((length, 4 * wide)), small(rate.shape), small(taps.shape)],
        out_shape=[
            jax.ShapeDtypeStruct((length, 4 * wide), HALF),
            jax.ShapeDtypeStruct(rate.shape, SINGLE),
            jax.ShapeDtypeStruct(taps.shape, SINGLE),
        ],
        scratch_shapes=[pltpu.VMEM((length, wide), SINGLE)],
        compiler_params=pltpu.CompilerParams(vmem_limit_bytes=48 * 1024 * 1024),
        cost_estimate=pl.CostEstimate(flops=12000000000, bytes_accessed=8000000, transcendentals=0),
        name="attend_back",
    )(qkv, w, raw, rate, taps, marks, segc, segr, grads, tri, carried, probs)


def leave_kernel(part, half, *refs):
    place_ref, rows_ref, gain_ref = refs[:3]
    group_refs = refs[3:7]
    own_refs = refs[7:11]
    other_refs = refs[11:15]
    attended_ref, middle_ref, normed_ref = refs[15:]
    for i in range(4):
        at = pl.multiple_of(place_ref[i] * part, part)
        attended_ref[:, pl.ds(at, part)] = group_refs[i][...]
    own_at = pl.multiple_of(place_ref[4], half)
    other_at = pl.multiple_of(half - place_ref[4], half)
    for at, pieces in ((own_at, own_refs), (other_at, other_refs)):
        total = mm(attended_ref[:, :part], pieces[0][...])
        for r in range(1, 4):
            total = total + mm(attended_ref[:, r * part : (r + 1) * part], pieces[r][...])
        middle_ref[:, pl.ds(at, half)] = rows_ref[:, pl.ds(at, half)] + total
    middle = middle_ref[...]
    inverse = lax.rsqrt(jnp.mean(middle * middle, axis=-1, keepdims=True) + EPS)
    normed_ref[...] = (middle * inverse * gain_ref[...]).astype(HALF)


def leave_attention(places, rows, gain, groups, own, other):
    length, width = rows.shape
    vmem = pl.BlockSpec(memory_space=pltpu.VMEM)
    return pl.pallas_call(
        functools.partial(leave_kernel, width // 4, width // 2),
        in_specs=[pl.BlockSpec(memory_space=pltpu.SMEM)] + [vmem] * 14,
        out_specs=[vmem] * 3,
        out_shape=[
            jax.ShapeDtypeStruct((length, width), HALF),
            jax.ShapeDtypeStruct((length, width), SINGLE),
            jax.ShapeDtypeStruct((length, width), HALF),
        ],
        compiler_params=pltpu.CompilerParams(vmem_limit_bytes=48 * 1024 * 1024),
        cost_estimate=pl.CostEstimate(flops=6000000000, bytes_accessed=14000000, transcendentals=0),
        name="leave_attention",
    )(places, rows, gain, *groups, *own, *other)


def return_kernel(part, half, *refs):
    place_ref, own_ref, last_ref, upstream_ref, middle_ref, gain_ref = refs[:6]
    own_refs = refs[6:10]
    other_refs = refs[10:14]
    middle_grad_ref, branch_ref, gain_grad_ref, group_ref = refs[14:]
    middle = middle_ref[...]
    inverse = lax.rsqrt(jnp.mean(middle * middle, axis=-1, keepdims=True) + EPS)
    unit = middle * inverse
    grad = own_ref[...] + last_ref[...].astype(SINGLE)
    gain_grad_ref[...] = jnp.sum(grad * unit, axis=0, keepdims=True)
    scaled = grad * gain_ref[...]
    middle_grad_ref[...] = upstream_ref[...].astype(SINGLE) + inverse * (
        scaled - unit * jnp.mean(scaled * unit, axis=-1, keepdims=True)
    )
    own_at = pl.multiple_of(place_ref[4], half)
    other_at = pl.multiple_of(half - place_ref[4], half)
    branch_ref[:, :half] = middle_grad_ref[:, pl.ds(own_at, half)].astype(HALF)
    branch_ref[:, half:] = middle_grad_ref[:, pl.ds(other_at, half)].astype(HALF)
    for r in range(4):
        total = mm_nt(branch_ref[:, :half], own_refs[r][...]) + mm_nt(branch_ref[:, half:], other_refs[r][...])
        group_ref[place_ref[5 + r]] = total.astype(HALF)


def return_to_attention(places, own_sum, last, upstream, middle, gain, own, other):
    length, width = middle.shape
    vmem = pl.BlockSpec(memory_space=pltpu.VMEM)
    return pl.pallas_call(
        functools.partial(return_kernel, width // 4, width // 2),
        in_specs=[pl.BlockSpec(memory_space=pltpu.SMEM)] + [vmem] * 13,
        out_specs=[vmem] * 4,
        out_shape=[
            jax.ShapeDtypeStruct((length, width), SINGLE),
            jax.ShapeDtypeStruct((length, width), HALF),
            jax.ShapeDtypeStruct((1, width), SINGLE),
            jax.ShapeDtypeStruct((4, length, width // 4), HALF),
        ],
        compiler_params=pltpu.CompilerParams(vmem_limit_bytes=48 * 1024 * 1024),
        cost_estimate=pl.CostEstimate(flops=6000000000, bytes_accessed=14000000, transcendentals=0),
        name="return_to_attention",
    )(places, own_sum, last, upstream, middle, gain, *own, *other)


AXES = ("grp", "fsdp")


def tie(*values):
    return lax.optimization_barrier(values)


def cut(array, start, size, axis):
    return lax.dynamic_slice_in_dim(array, start, size, axis)


def wide_sum(*terms):
    total = terms[0].astype(SINGLE)
    for term in terms[1:]:
        total = total + term.astype(SINGLE)
    return total


def turned(doc_row, taps_count):
    length = doc_row.shape[0]
    span = length // 2
    start = jnp.argmax(doc_row[: length - span + 1] == doc_row[span - 1 :])
    position = lax.iota(jnp.int32, length)
    source = (position + start) % length
    turn = (source[:, None] == position[None, :]).astype(HALF)
    segment = jnp.sum(jnp.where(turn > 0, doc_row[None, :], 0), axis=1)
    marks = jnp.stack(
        [((jnp.roll(segment, k) == segment) & (position >= k)).astype(SINGLE) for k in range(taps_count)],
        axis=1,
    )
    return turn, marks, segment[:, None], segment[None, :]


def turn_back(turn, array):
    high = array.astype(HALF)
    low = (array - high.astype(SINGLE)).astype(HALF)
    return mm_tn(turn, high) + mm_tn(turn, low)


def unit_norm(array):
    inverse = lax.rsqrt(jnp.mean(array * array, axis=-1, keepdims=True) + EPS)
    return array * inverse, inverse


def unit_back(grad, unit, inverse, gain):
    scaled = grad * gain
    return inverse * (scaled - unit * jnp.mean(scaled * unit, axis=-1, keepdims=True))


def gates(gate_rows, up_rows):
    gate_sig = jax.nn.sigmoid(gate_rows)
    return gate_sig, (gate_rows * gate_sig * up_rows).astype(HALF)


def gates_back(grad_hidden, gate_rows, up_rows, gate_sig):
    return jnp.concatenate(
        [
            (grad_hidden * up_rows * gate_sig * (1.0 + gate_rows * (1.0 - gate_sig))).astype(HALF),
            (grad_hidden * gate_rows * gate_sig).astype(HALF),
        ],
        axis=1,
    )


def local_any(
    tokens, doc_ids, cotangent, gain_in, w_query, w_key, w_value, w_house, w_rate, conv_taps, w_out,
    gain_mid, w_gate, w_up, w_down,
):
    heads = w_rate.shape[1]
    width = tokens.shape[2]
    dim = width // heads
    span = tokens.shape[1] // 2
    count = heads // 4
    wide = count * dim

    def fetch(array, axis=0):
        return lax.all_gather(array.astype(HALF), "fsdp", axis=axis, tiled=True)

    def share(array, axis=0):
        part = lax.psum_scatter(array.astype(HALF), "fsdp", scatter_dimension=axis, tiled=True)
        return lax.psum(part, "grp").astype(SINGLE)

    gain_first = fetch(gain_in).astype(SINGLE)
    gain_second = fetch(gain_mid).astype(SINGLE)
    projections = [fetch(w) for w in (w_query, w_key, w_value, w_house)]
    mat_rate = fetch(w_rate)
    tap_values = fetch(conv_taps, 1).astype(SINGLE)
    mat_out, mat_gate, mat_up, mat_down = [fetch(w) for w in (w_out, w_gate, w_up, w_down)]
    turn, marks, segc, segr = turned(doc_ids[0], conv_taps.shape[0])
    rows = mm(turn, tokens[0])
    upstream = mm(turn, cotangent[0]).astype(HALF)
    unit_in, inverse_in = unit_norm(rows)
    normed = (unit_in * gain_first).astype(HALF)
    rate_sig = jax.nn.sigmoid(
        lax.dot_general(mat_rate, normed, (((0,), (1,)), ((), ())), preferred_element_type=SINGLE)
    )
    rates = [2.0 * rate_sig[k * count : (k + 1) * count] for k in range(4)]
    taps = [tap_values[:, k * wide : (k + 1) * wide] for k in range(4)]
    pieces = [
        jnp.concatenate([w[:, k * wide : (k + 1) * wide] for w in projections], axis=1) for k in range(4)
    ]
    kept = [
        attn_forward(normed, [pieces[k]], rates[k], taps[k], marks, segc, segr, dim, span) for k in range(4)
    ]
    attended = jnp.concatenate([k[0] for k in kept], axis=1)
    middle = rows + mm(attended, mat_out)
    unit_mid, inverse_mid = unit_norm(middle)
    normed_mid = (unit_mid * gain_second).astype(HALF)
    gate_rows = mm(normed_mid, mat_gate)
    up_rows = mm(normed_mid, mat_up)
    gate_sig, hidden = gates(gate_rows, up_rows)
    result = (middle + mm(hidden, mat_down)).astype(HALF)
    feed_rows = gates_back(mm_nt(upstream, mat_down), gate_rows, up_rows, gate_sig)
    units = feed_rows.shape[1] // 2
    grad_gate_rows, grad_up_rows = feed_rows[:, :units], feed_rows[:, units:]
    grad_normed_mid = mm_nt(grad_gate_rows, mat_gate) + mm_nt(grad_up_rows, mat_up)
    grad_middle = upstream.astype(SINGLE) + unit_back(grad_normed_mid, unit_mid, inverse_mid, gain_second)
    grad_branch = grad_middle.astype(HALF)
    grad_att = mm_nt(grad_branch, mat_out).astype(HALF)
    row_grads, rate_grads, tap_grads = [], [], []
    for k in range(4):
        unused_out, qkv, raw, house, tri, carried, probs = kept[k]
        got = attn_backward(
            qkv, house, raw, rates[k], taps[k], marks, segc, segr, grad_att[None, :, k * wide : (k + 1) * wide], 0,
            tri, carried, probs, dim, span,
        )
        row_grads.append(got[0])
        rate_grads.append(got[1])
        tap_grads.append(got[2])
    grad_rate_rows = (jnp.concatenate(rate_grads, axis=0) * 2.0 * rate_sig * (1.0 - rate_sig)).astype(HALF)
    grad_normed = lax.dot_general(
        grad_rate_rows, mat_rate, (((0,), (1,)), ((), ())), preferred_element_type=SINGLE
    )
    for k in range(4):
        grad_normed = grad_normed + mm_nt(row_grads[k], pieces[k])
    grad_tokens = grad_middle + unit_back(grad_normed, unit_in, inverse_in, gain_first)
    weight_grads = []
    for m in range(4):
        part = jnp.concatenate([r[:, m * wide : (m + 1) * wide] for r in row_grads], axis=1)
        weight_grads.append(share(mm_tn(normed, part)))
    return (
        mm_tn(turn, result).astype(HALF)[None],
        turn_back(turn, grad_tokens)[None],
        share(jnp.sum(grad_normed * unit_in, axis=0)),
        weight_grads[0],
        weight_grads[1],
        weight_grads[2],
        weight_grads[3],
        share(lax.dot_general(normed, grad_rate_rows, (((0,), (1,)), ((), ())), preferred_element_type=SINGLE)),
        share(jnp.concatenate(tap_grads, axis=1), 1),
        share(mm_tn(attended, grad_branch)),
        share(jnp.sum(grad_normed_mid * unit_mid, axis=0)),
        share(mm_tn(normed_mid, grad_gate_rows)),
        share(mm_tn(normed_mid, grad_up_rows)),
        share(mm_tn(hidden, upstream)),
    )


class Links:
    def __init__(self, groups, shards):
        self.core = lax.axis_index("grp") % 2
        self.me = lax.axis_index("fsdp")
        near = 1 + self.core
        self.order = [self.me, self.me ^ near, self.me ^ (3 - near), self.me ^ 3]

        def permutation(move):
            pairs = []
            for g in range(groups):
                for f in range(shards):
                    target = move(g // 2, g % 2, f)
                    if target is not None:
                        pairs.append((g * shards + f, target[0] * shards + target[1]))
            return pairs

        self.pairs = {
            "near": permutation(lambda z, c, f: (2 * z + c, f ^ (1 + c))),
            "next": permutation(lambda z, c, f: (2 * z + c, f ^ (2 - c))),
            "twin": permutation(lambda z, c, f: (2 * z + 1 - c, f)),
            "inward": permutation(lambda z, c, f: (2 * (z ^ 1) + c, f) if z in (0, 3) else None),
            "across": permutation(lambda z, c, f: (2 * (3 - z) + c, f) if z in (1, 2) else None),
            "outward": permutation(lambda z, c, f: (2 * (z ^ 1) + c, f) if z in (1, 2) else None),
        }
        level = lax.axis_index("grp") // 2
        self.edge = (level == 0) | (level == 3)

    def near(self, array):
        return lax.ppermute(array, AXES, self.pairs["near"])

    def next(self, array):
        return lax.ppermute(array, AXES, self.pairs["next"])

    def twin(self, array):
        return lax.ppermute(array, AXES, self.pairs["twin"])

    def inward(self, array):
        return lax.ppermute(array, AXES, self.pairs["inward"])

    def across(self, array):
        return lax.ppermute(array, AXES, self.pairs["across"])

    def outward(self, array):
        return lax.ppermute(array, AXES, self.pairs["outward"])

    def settled(self, total, got):
        return jnp.where(self.edge, got, total)

    def place(self, number):
        apart = number ^ self.me
        return jnp.where((apart == 0) | (apart == 3) | (self.core == 0), apart, 3 - apart)

    def in_place(self, blocks):
        rows = blocks[0].shape[0]
        every = jnp.zeros((rows * 4,) + blocks[0].shape[1:], blocks[0].dtype)
        for number, block in zip(self.order, blocks):
            every = lax.dynamic_update_slice(every, block, (number * rows,) + (0,) * (block.ndim - 1))
        return every

    def by_core(self, own, other, axis):
        return jnp.where(
            self.core == 0,
            jnp.concatenate([own, other], axis=axis),
            jnp.concatenate([other, own], axis=axis),
        )


def core_sum(own, got):
    rows = own.shape[0] // 4
    flip = [got[i * rows : (i + 1) * rows] for i in (0, 2, 1, 3)]
    head = wide_sum(own[: 2 * rows], jnp.concatenate(flip[:2], axis=0)).astype(HALF)
    tail = wide_sum(own[2 * rows :], jnp.concatenate(flip[2:], axis=0)).astype(HALF)
    return head, tail


def second_sum(head, got):
    rows = head.shape[0] // 2
    return wide_sum(head[:rows], got[:rows]), wide_sum(head[rows:], got[rows:]).astype(HALF)


def local_paired(
    tokens, doc_ids, cotangent, gain_in, w_query, w_key, w_value, w_house, w_rate, conv_taps, w_out,
    gain_mid, w_gate, w_up, w_down, *, groups, shards,
):
    links = Links(groups, shards)
    core = links.core
    length = tokens.shape[1]
    width = tokens.shape[2]
    span = length // 2
    heads = w_rate.shape[1]
    dim = width // heads
    taps_count = conv_taps.shape[0]
    part = width // shards
    half_width = width // 2
    count = heads // 4
    wide = count * dim
    own_at = core * half_width
    other_at = half_width - own_at
    number = [2 * core, 2 * core + 1, 2 - 2 * core, 3 - 2 * core]
    hidden_part = w_gate.shape[1] // shards
    h = hidden_part // 2
    hid_own = core * h
    hid_other = h - hid_own

    def group_columns(k):
        return jnp.concatenate(
            [cut(matrix, k * wide, wide, 1).astype(HALF) for matrix in (w_query, w_key, w_value, w_house)],
            axis=1,
        )

    def feed_block(i):
        start = i * hidden_part + hid_own
        return jnp.concatenate([cut(w_gate, start, h, 1), cut(w_up, start, h, 1)], axis=1).astype(HALF)

    def in_order(array, axis):
        return jnp.concatenate([cut(array, i * part, part, axis) for i in links.order], axis=axis)

    def from_order(array, axis):
        return jnp.concatenate([cut(array, links.place(i) * part, part, axis) for i in range(4)], axis=axis)

    small = jnp.concatenate([gain_in[:, None], gain_mid[:, None], conv_taps.T, w_rate], axis=1).astype(HALF)
    small = jnp.pad(small, ((0, 0), (0, 128 - small.shape[1])))
    small_near, small_second = links.near(small), links.next(small)
    block0 = group_columns(number[0])
    near0, second0 = links.near(block0), links.next(block0)

    turn, marks, segc, segr = turned(doc_ids[0], taps_count)
    rows = mm(turn, tokens[0])
    unit_in, inverse_in = unit_norm(rows)
    unit_in = in_order(unit_in, 1)
    block1 = group_columns(number[1])

    near0, second0, small_near, small_second, block1, unit_in = tie(
        near0, second0, small_near, small_second, block1, unit_in
    )
    small_far = links.next(small_near)
    far0 = links.next(near0)
    twin0 = [links.twin(second0), links.twin(near0)]
    block2 = group_columns(number[2])
    small = [small, small_near, small_second, small_far]
    small_order = jnp.concatenate(small, axis=0)
    small_plain = links.in_place(small)
    gain_first = small_order[:, 0].astype(SINGLE)
    gain_second = small_plain[:, 1].astype(SINGLE)
    tap_values = small_plain[:, 2 : 2 + taps_count].astype(SINGLE)
    mat_rate = small_order[:, 2 + taps_count : 2 + taps_count + heads]
    normed = (unit_in * gain_first).astype(HALF)
    rate_sig = jax.nn.sigmoid(
        lax.dot_general(mat_rate, normed, (((0,), (1,)), ((), ())), preferred_element_type=SINGLE)
    )
    rates = [cut(2.0 * rate_sig, k * count, count, 0) for k in number]
    taps = [cut(tap_values, k * wide, wide, 0).T for k in number]
    normed, far0, block1, block2, *rest = tie(normed, far0, block1, block2, *rates, *taps)
    rates, taps = rest[:4], rest[4:]

    def forward(i, normed, pieces):
        return attn_forward(normed, pieces, rates[i], taps[i], marks, segc, segr, dim, span)

    kept = [None] * 4
    pieces = [None] * 4
    pieces[0] = [block0, near0, second0, far0]
    twin0.append(links.twin(far0))
    near1, second1 = links.near(block1), links.next(block1)
    kept[0] = forward(0, normed, pieces[0])

    normed, unused, *twin0 = tie(normed, kept[0][0], *twin0)
    pieces[2] = [block2] + twin0
    kept[2] = forward(2, normed, pieces[2])

    out_block = cut(w_out, own_at, half_width, 1).astype(HALF)
    near1, second1, normed, unused, out_block = tie(near1, second1, normed, kept[2][0], out_block)
    far1 = links.next(near1)
    out_near, out_second = links.near(out_block), links.next(out_block)
    twin1 = [links.twin(second1), links.twin(near1)]
    upstream = mm(turn, cotangent[0]).astype(HALF)
    block3 = group_columns(number[3])
    out_rest = cut(w_out, other_at, half_width, 1).astype(HALF)
    feed_first, feed_second, feed_far = [feed_block(i) for i in links.order[1:]]

    far1, normed, block3, feed_first, feed_second, feed_far, upstream, out_rest = tie(
        far1, normed, block3, feed_first, feed_second, feed_far, upstream, out_rest
    )
    twin1.append(links.twin(far1))
    pieces[1] = [block1, near1, second1, far1]
    feed_passing = links.near(feed_far)
    feed_next = links.next(feed_second)
    kept[1] = forward(1, normed, pieces[1])

    normed, unused, out_near, out_second, *twin1 = tie(normed, kept[1][0], out_near, out_second, *twin1)
    pieces[3] = [block3] + twin1
    out_far = links.next(out_near)
    feed_near = links.near(feed_first)
    out_twin = [links.twin(out_second), links.twin(out_near)]
    kept[3] = forward(3, normed, pieces[3])

    att3, out_far, feed_passing, *out_twin = tie(kept[3][0], out_far, feed_passing, *out_twin)
    feed_last = links.next(feed_passing)
    out_twin.append(links.twin(out_far))
    places = [links.place(k) for k in number] + [own_at] + [k ^ (2 * core) for k in links.order]
    places = jnp.stack([jnp.asarray(p, jnp.int32) for p in places])
    gain_second = gain_second[None, :]
    out_own = [out_block, out_near, out_second, out_far]
    out_other = [out_rest] + out_twin
    attended, middle, normed_mid = leave_attention(
        places, rows, gain_second, [kept[0][0], kept[1][0], kept[2][0], att3], out_own, out_other
    )

    mid_near, mid_second = links.near(normed_mid), links.next(normed_mid)
    feed_own = links.in_place([feed_block(links.me), feed_near, feed_next, feed_last])
    mat_down = jnp.concatenate(
        [cut(w_down, hid_own, h, 0), cut(w_down, hid_other, h, 0)], axis=0
    ).astype(HALF)
    mid_near, mid_second, feed_own, mat_down = tie(mid_near, mid_second, feed_own, mat_down)
    feed_other = links.twin(feed_own)
    mid_far = links.next(mid_near)
    up_near, up_second = links.near(upstream), links.next(upstream)
    mat_feed = jnp.concatenate(
        [feed_own[:, :h], feed_other[:, :h], feed_own[:, h:], feed_other[:, h:]], axis=1
    )
    mat_feed, mid_far = tie(mat_feed, mid_far)
    normed_all = jnp.concatenate([normed_mid, mid_near, mid_second, mid_far], axis=0)
    gate_up = mm(normed_all, mat_feed)
    up_near, up_second, gate_up = tie(up_near, up_second, gate_up)
    up_far = links.next(up_near)
    gate_rows, up_rows = gate_up[:, :hidden_part], gate_up[:, hidden_part:]
    gate_sig, hidden = gates(gate_rows, up_rows)
    down_tail = mm(hidden[2 * length :], mat_down).astype(HALF)
    up_far, down_tail, hidden = tie(up_far, down_tail, hidden)
    down_part = links.next(down_tail)
    upstream_all = jnp.concatenate([upstream, up_near, up_second, up_far], axis=0)
    grad_hidden = mm_nt(upstream_all, mat_down)
    feed_rows = gates_back(grad_hidden, gate_rows, up_rows, gate_sig)
    mid_tail = mm_nt(feed_rows[2 * length :], mat_feed).astype(HALF)

    mid_tail, feed_rows, hidden = tie(mid_tail, feed_rows, hidden)
    mid_got = links.next(mid_tail)
    grad_down = mm_tn(hidden, upstream_all).astype(HALF)
    down_head = mm(hidden[: 2 * length], mat_down)
    grad_down, feed_rows = tie(grad_down, feed_rows)
    down_got = links.twin(grad_down[h:])
    mid_head = mm_nt(feed_rows[: 2 * length], mat_feed)
    mid_got, mid_head, down_got, down_part, down_head = tie(mid_got, mid_head, down_got, down_part, down_head)
    mid_own, mid_first = second_sum(mid_head, mid_got)
    mid_last = links.near(mid_first)
    down_own, down_first = second_sum(down_head, down_part)
    down_sum = wide_sum(grad_down[:h], down_got).astype(HALF)
    down_in = links.inward(down_sum)
    grad_feed = mm_tn(normed_all, feed_rows).astype(HALF)

    mid_last, grad_feed, down_first, mid_own = tie(mid_last, grad_feed, down_first, mid_own)
    feed_got = links.twin(jnp.concatenate([grad_feed[:, h : 2 * h], grad_feed[:, 3 * h :]], axis=1))
    down_last = links.near(down_first)
    grad_middle, branch_pair, grad_gain_mid, grad_att = return_to_attention(
        places, mid_own, mid_last, upstream, middle, gain_second, out_own, out_other
    )
    out_grads = mm_tn(attended, branch_pair).astype(HALF)

    def backward(i, grad_att):
        unused_out, qkv, raw, house, tri, carried, probs = kept[i]
        return attn_backward(
            qkv, house, raw, rates[i], taps[i], marks, segc, segr, grad_att, i, tri, carried, probs, dim, span
        )

    row_grads = [None] * 4
    rate_grads = [None] * 4
    tap_grads = [None] * 4
    out_grads, feed_got, grad_att = tie(out_grads, feed_got, grad_att)
    out_got = links.twin(out_grads[:, half_width:])
    feed_sum = wide_sum(
        jnp.concatenate([grad_feed[:, :h], grad_feed[:, 2 * h : 3 * h]], axis=1), feed_got
    ).astype(HALF)
    feed0, feed1 = feed_sum[: width // 2], feed_sum[width // 2 :]
    row_grads[2], rate_grads[2], tap_grads[2] = backward(2, grad_att)
    other = mm_tn(normed, row_grads[2]).astype(HALF)

    other, out_got, grad_att, down_in, feed0, feed1 = tie(other, out_got, grad_att, down_in, feed0, feed1)
    got0 = links.twin(other)
    feed0_in = links.inward(feed0)
    down_sum = wide_sum(down_sum, down_in).astype(HALF)
    down_across = links.across(down_sum)
    out_head, out_tail = core_sum(out_grads[:, :half_width], out_got)
    out_part = links.next(out_tail)
    row_grads[0], rate_grads[0], tap_grads[0] = backward(0, grad_att)
    own0 = mm_tn(normed, row_grads[0]).astype(HALF)

    own0, got0, out_part, grad_att, down_last = tie(own0, got0, out_part, grad_att, down_last)
    head0, tail0 = core_sum(own0, got0)
    part0 = links.next(tail0)
    out_own_sum, out_first = second_sum(out_head, out_part)
    out_last = links.near(out_first)
    row_grads[3], rate_grads[3], tap_grads[3] = backward(3, grad_att)
    other = mm_tn(normed, row_grads[3]).astype(HALF)

    other, out_last, grad_att, feed0_in, down_across = tie(other, out_last, grad_att, feed0_in, down_across)
    got1 = links.twin(other)
    feed1_in = links.inward(feed1)
    feed0 = wide_sum(feed0, feed0_in).astype(HALF)
    feed0_across = links.across(feed0)
    down_sum = wide_sum(down_sum, down_across).astype(HALF)
    down_out = links.outward(down_sum)
    out_sum = wide_sum(out_own_sum, out_last).astype(HALF)
    result = (middle + wide_sum(down_own, down_last)).astype(HALF)
    result = mm_tn(turn, result).astype(HALF)
    row_grads[1], rate_grads[1], tap_grads[1] = backward(1, grad_att)
    own1 = mm_tn(normed, row_grads[1]).astype(HALF)

    own1, got1, part0, out_sum = tie(own1, got1, part0, out_sum)
    sum0, first0 = second_sum(head0, part0)
    last0 = links.near(first0)
    head1, tail1 = core_sum(own1, got1)
    part1 = links.next(tail1)

    grad_rate = links.by_core(
        jnp.concatenate(rate_grads[:2], axis=0), jnp.concatenate(rate_grads[2:], axis=0), 0
    )
    grad_taps = links.by_core(
        jnp.concatenate(tap_grads[:2], axis=1), jnp.concatenate(tap_grads[2:], axis=1), 1
    )
    grad_rate_rows = (grad_rate * 2.0 * rate_sig * (1.0 - rate_sig)).astype(HALF)
    grad_wrate = lax.dot_general(
        normed, grad_rate_rows, (((0,), (1,)), ((), ())), preferred_element_type=SINGLE
    )
    grad_normed = lax.dot_general(
        grad_rate_rows, mat_rate, (((0,), (1,)), ((), ())), preferred_element_type=SINGLE
    )
    for i in (0, 2):
        grad_normed = grad_normed + mm_nt(row_grads[i], jnp.concatenate(pieces[i], axis=0))

    feed1_in, feed0_across, last0, grad_normed, down_out = tie(feed1_in, feed0_across, last0, grad_normed, down_out)
    feed1 = wide_sum(feed1, feed1_in).astype(HALF)
    feed1_across = links.across(feed1)
    feed0 = wide_sum(feed0, feed0_across).astype(HALF)
    feed0_out = links.outward(feed0)
    out_in = links.inward(out_sum)
    sum0 = wide_sum(sum0, last0).astype(HALF)
    sum0_in = links.inward(sum0)
    down_sum = links.settled(down_sum, down_out)
    down_twin = links.twin(down_sum)
    for i in (1, 3):
        grad_normed = grad_normed + mm_nt(row_grads[i], jnp.concatenate(pieces[i], axis=0))
    grad_gain_in = jnp.sum(grad_normed * unit_in, axis=0)
    extra = jnp.concatenate(
        [grad_gain_in[:, None], in_order(grad_gain_mid[0], 0)[:, None], in_order(grad_taps.T, 0), grad_wrate],
        axis=1,
    )
    extra = jnp.pad(extra, ((0, 0), (0, 128 - extra.shape[1]))).astype(HALF)

    extra, part1, out_in, grad_normed = tie(extra, part1, out_in, grad_normed)
    extra_got = links.twin(extra)
    sum1, first1 = second_sum(head1, part1)
    last1 = links.near(first1)
    out_sum = wide_sum(out_sum, out_in).astype(HALF)
    out_across = links.across(out_sum)
    norm_grad = unit_back(grad_normed, unit_in, inverse_in, gain_first)
    grad_tokens = turn_back(turn, grad_middle + from_order(norm_grad, 1))

    grad_tokens, feed1_across, sum0_in, extra_got, last1, feed0_out = tie(
        grad_tokens, feed1_across, sum0_in, extra_got, last1, feed0_out
    )
    feed1 = wide_sum(feed1, feed1_across).astype(HALF)
    feed1_out = links.outward(feed1)
    sum0 = wide_sum(sum0, sum0_in).astype(HALF)
    sum0_across = links.across(sum0)
    sum1 = wide_sum(sum1, last1).astype(HALF)
    sum1 = [sum1[: part // 2], sum1[part // 2 :]]
    sum1_in = [links.inward(a) for a in sum1]
    extra_head, extra_tail = core_sum(extra, extra_got)
    extra_part = links.next(extra_tail)
    grad_down = links.by_core(down_sum, down_twin, 0).astype(SINGLE)
    feed0 = links.settled(feed0, feed0_out)

    feed1_out, sum0_across, out_across, extra_part, grad_down, feed0, *sum1_in = tie(
        feed1_out, sum0_across, out_across, extra_part, grad_down, feed0, *sum1_in
    )
    sum0 = wide_sum(sum0, sum0_across).astype(HALF)
    sum0_out = links.outward(sum0)
    sum1 = [wide_sum(a, b).astype(HALF) for a, b in zip(sum1, sum1_in)]
    sum1_across = [links.across(a) for a in sum1]
    out_sum = wide_sum(out_sum, out_across).astype(HALF)
    out_out = links.outward(out_sum)
    feed_sum = jnp.concatenate([feed0, links.settled(feed1, feed1_out)], axis=0)
    feed_blocks = [cut(feed_sum, i * part, part, 0) for i in links.order]
    feed_passing, feed_near = links.near(feed_blocks[3]), links.near(feed_blocks[1])
    feed_next = links.next(feed_blocks[2])
    extra_own, extra_first = second_sum(extra_head, extra_part)
    extra_sum = wide_sum(extra_own, links.near(extra_first)).astype(HALF)
    extra_in = links.inward(extra_sum)

    feed_passing, out_out, sum0_out, extra_in, *sum1_across = tie(
        feed_passing, out_out, sum0_out, extra_in, *sum1_across
    )
    feed_last = links.next(feed_passing)
    sum1 = [wide_sum(a, b).astype(HALF) for a, b in zip(sum1, sum1_across)]
    sum1_out = [links.outward(a) for a in sum1]
    out_sum = links.settled(out_sum, out_out)
    out_twin = links.twin(out_sum)
    sum0 = links.settled(sum0, sum0_out)
    twin0 = links.twin(sum0)
    extra_sum = wide_sum(extra_sum, extra_in).astype(HALF)
    extra_across = links.across(extra_sum)
    grad_wout = links.by_core(out_sum, out_twin, 1).astype(SINGLE)

    feed_last, extra_across, *sum1_out = tie(feed_last, extra_across, *sum1_out)
    feed_mine = links.in_place([feed_blocks[0], feed_near, feed_next, feed_last])
    feed_twin = links.twin(feed_mine)
    sum1 = jnp.concatenate([links.settled(a, b) for a, b in zip(sum1, sum1_out)], axis=0)
    twin1 = links.twin(sum1)
    extra_sum = wide_sum(extra_sum, extra_across).astype(HALF)
    extra = links.settled(extra_sum, links.outward(extra_sum)).astype(SINGLE)

    grad_gate, grad_up = [
        jnp.concatenate(
            [
                links.by_core(
                    feed_mine[i * part : (i + 1) * part, at : at + h],
                    feed_twin[i * part : (i + 1) * part, at : at + h],
                    1,
                )
                for i in range(shards)
            ],
            axis=1,
        ).astype(SINGLE)
        for at in (0, h)
    ]
    sums = [(sum0, twin0), (sum1, twin1)]
    weight_grads = []
    for m in range(4):
        columns = [[a[:, m * wide : (m + 1) * wide] for a in pair] for pair in sums]
        weight_grads.append(
            links.by_core(
                jnp.concatenate([columns[0][0], columns[1][0]], axis=1),
                jnp.concatenate([columns[0][1], columns[1][1]], axis=1),
                1,
            ).astype(SINGLE)
        )

    return (
        result[None],
        grad_tokens[None],
        extra[:, 0],
        weight_grads[0],
        weight_grads[1],
        weight_grads[2],
        weight_grads[3],
        extra[:, 2 + taps_count : 2 + taps_count + heads],
        extra[:, 2 : 2 + taps_count].T,
        grad_wout,
        extra[:, 1],
        grad_gate,
        grad_up,
        grad_down,
    )


def solution(mesh):
    groups, shards = mesh.shape["grp"], mesh.shape["fsdp"]
    if (groups, shards) == (8, 4):
        body = functools.partial(local_paired, groups=groups, shards=shards)
    else:
        body = local_any
    rows = P(("grp", "fsdp"), None, None)
    vector = P("fsdp")
    matrix = P("fsdp", None)
    taps = P(None, "fsdp")
    return jax.shard_map(
        body,
        mesh=mesh,
        in_specs=(
            rows, P(("grp", "fsdp"), None), rows, vector, matrix, matrix, matrix, matrix, matrix,
            taps, matrix, vector, matrix, matrix, matrix,
        ),
        out_specs=(
            rows, rows, vector, matrix, matrix, matrix, matrix, matrix, taps, matrix, vector,
            matrix, matrix, matrix,
        ),
        check_vma=False,
    )
```

```python
import functools
import jax
import jax.numpy as jnp
from jax import lax
from jax.experimental import pallas as pl
from jax.experimental.pallas import tpu as pltpu
from jax.sharding import PartitionSpec as P

EPS = 1e-06
HALF = jnp.bfloat16
SINGLE = jnp.float32


def mm(left, right):
    return lax.dot_general(left, right, (((1,), (0,)), ((), ())), preferred_element_type=SINGLE)


def mm_nt(left, right):
    return lax.dot_general(left, right, (((1,), (1,)), ((), ())), preferred_element_type=SINGLE)


def mm_tn(left, right):
    return lax.dot_general(left, right, (((0,), (0,)), ((), ())), preferred_element_type=SINGLE)


def conv_parts(raw, taps, marks, taps_count):
    shifted = [raw]
    total = raw * taps[0:1, :]
    for k in range(1, taps_count):
        moved = pltpu.roll(raw, k, 0) * marks[:, k : k + 1]
        shifted.append(moved)
        total = total + moved * taps[k : k + 1, :]
    return shifted, total


def attn_forward_kernel(
    span, dim, count, taps_count, number, *refs
):
    normed_ref = refs[0]
    piece_refs = refs[1 : 1 + number]
    rate_ref, taps_ref, marks_ref, segc_ref, segr_ref = refs[1 + number : 6 + number]
    out_ref, qkv_ref, raw_ref, w_ref, t_ref, c_ref, p_ref = refs[6 + number :]
    blocks = normed_ref.shape[0] // span
    wide = count * dim
    depth = normed_ref.shape[1] // number
    for m in (3, 0, 1, 2):
        total = mm(normed_ref[:, :depth], piece_refs[0][:, m * wide : (m + 1) * wide])
        for r in range(1, number):
            total = total + mm(
                normed_ref[:, r * depth : (r + 1) * depth], piece_refs[r][:, m * wide : (m + 1) * wide]
            )
        if m == 3:
            raw_ref[...] = total
        else:
            qkv_ref[:, m * wide : (m + 1) * wide] = total.astype(HALF)
    q_ref, k_ref, v_ref = [qkv_ref.at[:, m * wide : (m + 1) * wide] for m in range(3)]
    marks = marks_ref[...]
    row_id = lax.broadcasted_iota(jnp.int32, (span, span), 0)
    col_id = lax.broadcasted_iota(jnp.int32, (span, span), 1)
    eye = jnp.where(row_id == col_id, 1.0, 0.0)
    sizes = []
    size = 1
    while size < span:
        sizes.append(size)
        size *= 2
    level_of = {}
    for size in sizes:
        level_of[size] = ((row_id // (2 * size)) == (col_id // (2 * size))) & (
            (row_id // size) > (col_id // size)
        )
    strict = []
    inclusive = []
    for u in range(blocks):
        rows = slice(u * span, (u + 1) * span)
        same = segc_ref[rows, 0:1] == segr_ref[0:1, rows]
        strict.append(same & (col_id < row_id))
        inclusive.append(same & (col_id <= row_id))
    for h in range(count):
        cols = slice(h * dim, (h + 1) * dim)
        shifted, mixed = conv_parts(raw_ref[:, cols], taps_ref[:, cols], marks, taps_count)
        inverse = lax.rsqrt(jnp.sum(mixed * mixed, axis=-1, keepdims=True) + EPS)
        w_ref[:, cols] = (mixed * inverse).astype(HALF)
    units = [(h, u) for h in range(count) for u in range(blocks)]
    rates = {}
    lower = {}
    inv = {}
    for h, u in units:
        rows = slice(u * span, (u + 1) * span)
        cols = slice(h * dim, (h + 1) * dim)
        w = w_ref[rows, cols]
        rates[h, u] = rate_ref[h : h + 1, rows]
        lw = jnp.where(strict[u], mm_nt(w, w) * rates[h, u], 0.0)
        lower[h, u] = lw.astype(HALF)
        inv[h, u] = eye - jnp.where(level_of[1], lw, 0.0)
    for size in sizes[1:]:
        half_inv = {}
        inner = {}
        for unit in units:
            half_inv[unit] = inv[unit].astype(HALF)
            inner[unit] = mm(jnp.where(level_of[size], lower[unit], jnp.zeros_like(lower[unit])), half_inv[unit])
        for unit in units:
            inv[unit] = inv[unit] - mm(half_inv[unit], inner[unit].astype(HALF))
    for h, u in units:
        rows = slice(u * span, (u + 1) * span)
        cols = slice(h * dim, (h + 1) * dim)
        w = w_ref[rows, cols]
        q = q_ref[rows, cols]
        k = k_ref[rows, cols]
        tri = inv[h, u].astype(HALF)
        t_ref[h * blocks + u] = tri
        right = jnp.where(strict[u], mm_nt(w, k), 0.0).astype(HALF)
        carried = mm(tri, right).astype(HALF)
        c_ref[h * blocks + u] = carried
        reach = (jnp.where(inclusive[u], mm_nt(q, w), 0.0) * rates[h, u]).astype(HALF)
        scores = (mm_nt(q, k) - mm(reach, carried)) * dim ** (-0.5)
        scores = jnp.where(inclusive[u], scores, -1e30)
        terms = jnp.exp(scores - jnp.max(scores, axis=1, keepdims=True))
        probs = (terms / jnp.sum(terms, axis=1, keepdims=True)).astype(HALF)
        p_ref[h * blocks + u] = probs
        out_ref[rows, cols] = mm(probs, v_ref[rows, cols]).astype(HALF)


def attn_backward_kernel(
    span, dim, count, taps_count,
    qkv_ref, w_ref, raw_ref, rate_ref, taps_ref, marks_ref, segc_ref, segr_ref, grad_ref, t_ref, c_ref, p_ref,
    out_ref, drate_ref, dtaps_ref, dw_ref,
):
    blocks = qkv_ref.shape[0] // span
    wide = count * dim
    q_ref, k_ref, v_ref = [qkv_ref.at[:, m * wide : (m + 1) * wide] for m in range(3)]
    dq_ref, dk_ref, dv_ref, draw_ref = [out_ref.at[:, m * wide : (m + 1) * wide] for m in range(4)]
    marks = marks_ref[...]
    row_id = lax.broadcasted_iota(jnp.int32, (span, span), 0)
    col_id = lax.broadcasted_iota(jnp.int32, (span, span), 1)
    scale = dim ** (-0.5)
    for u in range(blocks):
        rows = slice(u * span, (u + 1) * span)
        same = segc_ref[rows, 0:1] == segr_ref[0:1, rows]
        strict = same & (col_id < row_id)
        inclusive = same & (col_id <= row_id)
        for h in range(count):
            cols = slice(h * dim, (h + 1) * dim)
            unit = h * blocks + u
            q = q_ref[rows, cols]
            k = k_ref[rows, cols]
            v = v_ref[rows, cols]
            w = w_ref[rows, cols]
            grad = grad_ref[0, rows, cols]
            rate = rate_ref[h : h + 1, rows]
            probs = p_ref[unit]
            carried = c_ref[unit]
            tri = t_ref[unit]
            dprobs = mm_nt(grad, v)
            dv_ref[rows, cols] = mm_tn(probs, grad).astype(HALF)
            probs = probs.astype(SINGLE)
            weighted = probs * dprobs
            dscore = ((weighted - probs * jnp.sum(weighted, axis=1, keepdims=True)) * scale).astype(HALF)
            reach_raw = jnp.where(inclusive, mm_nt(q, w), 0.0)
            reach = (reach_raw * rate).astype(HALF)
            dreach = -mm_nt(dscore, carried)
            drate = jnp.sum(dreach * reach_raw, axis=0, keepdims=True)
            dreach = (jnp.where(inclusive, dreach, 0.0) * rate).astype(HALF)
            dcarried = (-mm_tn(reach, dscore)).astype(HALF)
            dright = jnp.where(strict, mm_tn(tri, dcarried), 0.0).astype(HALF)
            dlower = jnp.where(strict, -mm_nt(dright, carried), 0.0)
            drate = drate + jnp.sum(dlower * mm_nt(w, w), axis=0, keepdims=True)
            dlower = (dlower * rate).astype(HALF)
            dq_ref[rows, cols] = (mm(dscore, k) + mm(dreach, w)).astype(HALF)
            dk_ref[rows, cols] = (mm_tn(dscore, q) + mm_tn(dright, w)).astype(HALF)
            dw_ref[rows, cols] = mm_tn(dreach, q) + mm(dright, k) + mm(dlower, w) + mm_tn(dlower, w)
            drate_ref[h : h + 1, rows] = drate
    length = q_ref.shape[0]
    for h in range(count):
        cols = slice(h * dim, (h + 1) * dim)
        taps = taps_ref[:, cols]
        shifted, mixed = conv_parts(raw_ref[:, cols], taps, marks, taps_count)
        inverse = lax.rsqrt(jnp.sum(mixed * mixed, axis=-1, keepdims=True) + EPS)
        unit_rows = mixed * inverse
        dw = dw_ref[:, cols]
        dmixed = inverse * (dw - unit_rows * jnp.sum(dw * unit_rows, axis=-1, keepdims=True))
        draw = dmixed * taps[0:1, :]
        dtaps = [jnp.sum(dmixed * shifted[0], axis=0, keepdims=True)]
        for k in range(1, taps_count):
            dtaps.append(jnp.sum(dmixed * shifted[k], axis=0, keepdims=True))
            draw = draw + pltpu.roll(dmixed * marks[:, k : k + 1], length - k, 0) * taps[k : k + 1, :]
        draw_ref[:, cols] = draw.astype(HALF)
        dtaps_ref[:, cols] = jnp.concatenate(dtaps, axis=0)


def attn_forward(normed, pieces, rate, taps, marks, segc, segr, dim, span):
    length = normed.shape[0]
    count = rate.shape[0]
    wide = count * dim
    units = count * (length // span)
    square = jax.ShapeDtypeStruct((units, span, span), HALF)
    return pl.pallas_call(
        functools.partial(attn_forward_kernel, span, dim, count, taps.shape[0], len(pieces)),
        out_shape=[
            jax.ShapeDtypeStruct((length, wide), HALF),
            jax.ShapeDtypeStruct((length, 3 * wide), HALF),
            jax.ShapeDtypeStruct((length, wide), SINGLE),
            jax.ShapeDtypeStruct((length, wide), HALF),
            square, square, square,
        ],
        compiler_params=pltpu.CompilerParams(vmem_limit_bytes=60 * 1024 * 1024),
        cost_estimate=pl.CostEstimate(flops=16000000000, bytes_accessed=12000000, transcendentals=0),
        name="attend",
    )(normed, *pieces, rate, taps, marks, segc, segr)


def attn_backward(qkv, w, raw, rate, taps, marks, segc, segr, grads, group, tri, carried, probs, dim, span):
    length = qkv.shape[0]
    count = rate.shape[0]
    wide = count * dim
    whole = lambda a: pl.BlockSpec(a.shape, lambda g: (0,) * a.ndim)
    small = lambda shape: pl.BlockSpec(shape, lambda g: (0, 0))
    return pl.pallas_call(
        functools.partial(attn_backward_kernel, span, dim, count, taps.shape[0]),
        grid=(1,),
        in_specs=[whole(a) for a in (qkv, w, raw, rate, taps, marks, segc, segr)]
        + [pl.BlockSpec((1, length, wide), lambda g: (group, 0, 0))]
        + [whole(a) for a in (tri, carried, probs)],
        out_specs=[small((length, 4 * wide)), small(rate.shape), small(taps.shape)],
        out_shape=[
            jax.ShapeDtypeStruct((length, 4 * wide), HALF),
            jax.ShapeDtypeStruct(rate.shape, SINGLE),
            jax.ShapeDtypeStruct(taps.shape, SINGLE),
        ],
        scratch_shapes=[pltpu.VMEM((length, wide), SINGLE)],
        compiler_params=pltpu.CompilerParams(vmem_limit_bytes=60 * 1024 * 1024),
        cost_estimate=pl.CostEstimate(flops=12000000000, bytes_accessed=8000000, transcendentals=0),
        name="attend_back",
    )(qkv, w, raw, rate, taps, marks, segc, segr, grads, tri, carried, probs)


def leave_kernel(part, half, *refs):
    place_ref, rows_ref, gain_ref = refs[:3]
    group_refs = refs[3:7]
    own_refs = refs[7:11]
    other_refs = refs[11:15]
    attended_ref, middle_ref, normed_ref = refs[15:]
    for i in range(4):
        at = pl.multiple_of(place_ref[i] * part, part)
        attended_ref[:, pl.ds(at, part)] = group_refs[i][...]
    own_at = pl.multiple_of(place_ref[4], half)
    other_at = pl.multiple_of(half - place_ref[4], half)
    for at, pieces in ((own_at, own_refs), (other_at, other_refs)):
        total = mm(attended_ref[:, :part], pieces[0][...])
        for r in range(1, 4):
            total = total + mm(attended_ref[:, r * part : (r + 1) * part], pieces[r][...])
        middle_ref[:, pl.ds(at, half)] = rows_ref[:, pl.ds(at, half)] + total
    middle = middle_ref[...]
    inverse = lax.rsqrt(jnp.mean(middle * middle, axis=-1, keepdims=True) + EPS)
    normed_ref[...] = (middle * inverse * gain_ref[...]).astype(HALF)


def leave_attention(places, rows, gain, groups, own, other):
    length, width = rows.shape
    vmem = pl.BlockSpec(memory_space=pltpu.VMEM)
    return pl.pallas_call(
        functools.partial(leave_kernel, width // 4, width // 2),
        in_specs=[pl.BlockSpec(memory_space=pltpu.SMEM)] + [vmem] * 14,
        out_specs=[vmem] * 3,
        out_shape=[
            jax.ShapeDtypeStruct((length, width), HALF),
            jax.ShapeDtypeStruct((length, width), SINGLE),
            jax.ShapeDtypeStruct((length, width), HALF),
        ],
        compiler_params=pltpu.CompilerParams(vmem_limit_bytes=60 * 1024 * 1024),
        cost_estimate=pl.CostEstimate(flops=6000000000, bytes_accessed=14000000, transcendentals=0),
        name="leave_attention",
    )(places, rows, gain, *groups, *own, *other)


def return_kernel(part, half, *refs):
    place_ref, own_ref, last_ref, upstream_ref, middle_ref, gain_ref = refs[:6]
    own_refs = refs[6:10]
    other_refs = refs[10:14]
    middle_grad_ref, branch_ref, gain_grad_ref, group_ref = refs[14:]
    middle = middle_ref[...]
    inverse = lax.rsqrt(jnp.mean(middle * middle, axis=-1, keepdims=True) + EPS)
    unit = middle * inverse
    grad = own_ref[...] + last_ref[...].astype(SINGLE)
    gain_grad_ref[...] = jnp.sum(grad * unit, axis=0, keepdims=True)
    scaled = grad * gain_ref[...]
    middle_grad_ref[...] = upstream_ref[...].astype(SINGLE) + inverse * (
        scaled - unit * jnp.mean(scaled * unit, axis=-1, keepdims=True)
    )
    own_at = pl.multiple_of(place_ref[4], half)
    other_at = pl.multiple_of(half - place_ref[4], half)
    branch_ref[:, :half] = middle_grad_ref[:, pl.ds(own_at, half)].astype(HALF)
    branch_ref[:, half:] = middle_grad_ref[:, pl.ds(other_at, half)].astype(HALF)
    for r in range(4):
        total = mm_nt(branch_ref[:, :half], own_refs[r][...]) + mm_nt(branch_ref[:, half:], other_refs[r][...])
        group_ref[place_ref[5 + r]] = total.astype(HALF)


def return_to_attention(places, own_sum, last, upstream, middle, gain, own, other):
    length, width = middle.shape
    vmem = pl.BlockSpec(memory_space=pltpu.VMEM)
    return pl.pallas_call(
        functools.partial(return_kernel, width // 4, width // 2),
        in_specs=[pl.BlockSpec(memory_space=pltpu.SMEM)] + [vmem] * 13,
        out_specs=[vmem] * 4,
        out_shape=[
            jax.ShapeDtypeStruct((length, width), SINGLE),
            jax.ShapeDtypeStruct((length, width), HALF),
            jax.ShapeDtypeStruct((1, width), SINGLE),
            jax.ShapeDtypeStruct((4, length, width // 4), HALF),
        ],
        compiler_params=pltpu.CompilerParams(vmem_limit_bytes=60 * 1024 * 1024),
        cost_estimate=pl.CostEstimate(flops=6000000000, bytes_accessed=14000000, transcendentals=0),
        name="return_to_attention",
    )(places, own_sum, last, upstream, middle, gain, *own, *other)


def feed_forward_kernel(units, rows_ref, feed_ref, down_ref, both_ref, hidden_ref, part_ref):
    both_ref[...] = mm(rows_ref[...], feed_ref[...])
    gate = both_ref[:, :units]
    hidden_ref[...] = (gate * jax.nn.sigmoid(gate) * both_ref[:, units:]).astype(HALF)
    part_ref[...] = mm(hidden_ref[...], down_ref[...]).astype(HALF)


def feed_forward(rows, mat_feed, mat_down, blocks):
    total, width = rows.shape
    units = mat_down.shape[0]
    size = total // blocks
    by_rows = lambda columns: pl.BlockSpec((size, columns), lambda i: (i, 0))
    whole = lambda a: pl.BlockSpec(a.shape, lambda i: (0, 0))
    return pl.pallas_call(
        functools.partial(feed_forward_kernel, units),
        grid=(blocks,),
        in_specs=[by_rows(width), whole(mat_feed), whole(mat_down)],
        out_specs=[by_rows(2 * units), by_rows(units), by_rows(width)],
        out_shape=[
            jax.ShapeDtypeStruct((total, 2 * units), SINGLE),
            jax.ShapeDtypeStruct((total, units), HALF),
            jax.ShapeDtypeStruct((total, width), HALF),
        ],
        compiler_params=pltpu.CompilerParams(vmem_limit_bytes=60 * 1024 * 1024),
        cost_estimate=pl.CostEstimate(flops=18000000000, bytes_accessed=30000000, transcendentals=0),
        name="feed_forward",
    )(rows, mat_feed, mat_down)


def feed_backward_kernel(units, *refs):
    upstream_ref, both_ref, feed_ref, down_ref = refs[:4]
    rows_ref, part_ref = refs[-2:]
    grad = mm_nt(upstream_ref[...], down_ref[...])
    gate = both_ref[:, :units]
    up = both_ref[:, units:]
    sig = jax.nn.sigmoid(gate)
    rows_ref[:, units:] = (grad * gate * sig).astype(HALF)
    rows_ref[:, :units] = (grad * up * sig * (1.0 + gate * (1.0 - sig))).astype(HALF)
    part_ref[...] = mm_nt(rows_ref[...], feed_ref[...]).astype(HALF)


def feed_backward(upstream, both, mat_feed, mat_down, blocks, first, number, filled=None):
    total, width = upstream.shape
    units = mat_down.shape[0]
    size = total // blocks
    by_rows = lambda columns: pl.BlockSpec((size, columns), lambda i: (i + first, 0))
    whole = lambda a: pl.BlockSpec(a.shape, lambda i: (0, 0))
    more = [] if filled is None else [filled]
    return pl.pallas_call(
        functools.partial(feed_backward_kernel, units),
        grid=(number,),
        in_specs=[by_rows(width), by_rows(2 * units), whole(mat_feed), whole(mat_down)]
        + [pl.BlockSpec(memory_space=pl.ANY)] * len(more),
        out_specs=[by_rows(2 * units), pl.BlockSpec((size, width), lambda i: (i, 0))],
        out_shape=[
            jax.ShapeDtypeStruct((total, 2 * units), HALF),
            jax.ShapeDtypeStruct((size * number, width), HALF),
        ],
        input_output_aliases={4: 0} if more else {},
        compiler_params=pltpu.CompilerParams(vmem_limit_bytes=60 * 1024 * 1024),
        cost_estimate=pl.CostEstimate(flops=9000000000, bytes_accessed=25000000, transcendentals=0),
        name="feed_backward",
    )(upstream, both, mat_feed, mat_down, *more)


AXES = ("grp", "fsdp")


def tie(*values):
    return lax.optimization_barrier(values)


def cut(array, start, size, axis):
    return lax.dynamic_slice_in_dim(array, start, size, axis)


def wide_sum(*terms):
    total = terms[0].astype(SINGLE)
    for term in terms[1:]:
        total = total + term.astype(SINGLE)
    return total


def turned(doc_row, taps_count):
    length = doc_row.shape[0]
    span = length // 2
    start = jnp.argmax(doc_row[: length - span + 1] == doc_row[span - 1 :])
    position = lax.iota(jnp.int32, length)
    source = (position + start) % length
    turn = (source[:, None] == position[None, :]).astype(HALF)
    segment = jnp.sum(jnp.where(turn > 0, doc_row[None, :], 0), axis=1)
    marks = jnp.stack(
        [((jnp.roll(segment, k) == segment) & (position >= k)).astype(SINGLE) for k in range(taps_count)],
        axis=1,
    )
    return turn, marks, segment[:, None], segment[None, :]


def turn_back(turn, array):
    high = array.astype(HALF)
    low = (array - high.astype(SINGLE)).astype(HALF)
    return mm_tn(turn, high) + mm_tn(turn, low)


def unit_norm(array):
    inverse = lax.rsqrt(jnp.mean(array * array, axis=-1, keepdims=True) + EPS)
    return array * inverse, inverse


def unit_back(grad, unit, inverse, gain):
    scaled = grad * gain
    return inverse * (scaled - unit * jnp.mean(scaled * unit, axis=-1, keepdims=True))


def gates(gate_rows, up_rows):
    gate_sig = jax.nn.sigmoid(gate_rows)
    return gate_sig, (gate_rows * gate_sig * up_rows).astype(HALF)


def gates_back(grad_hidden, gate_rows, up_rows, gate_sig):
    return jnp.concatenate(
        [
            (grad_hidden * up_rows * gate_sig * (1.0 + gate_rows * (1.0 - gate_sig))).astype(HALF),
            (grad_hidden * gate_rows * gate_sig).astype(HALF),
        ],
        axis=1,
    )


def local_any(
    tokens, doc_ids, cotangent, gain_in, w_query, w_key, w_value, w_house, w_rate, conv_taps, w_out,
    gain_mid, w_gate, w_up, w_down,
):
    heads = w_rate.shape[1]
    width = tokens.shape[2]
    dim = width // heads
    span = tokens.shape[1] // 2
    count = heads // 4
    wide = count * dim

    def fetch(array, axis=0):
        return lax.all_gather(array.astype(HALF), "fsdp", axis=axis, tiled=True)

    def share(array, axis=0):
        part = lax.psum_scatter(array.astype(HALF), "fsdp", scatter_dimension=axis, tiled=True)
        return lax.psum(part, "grp").astype(SINGLE)

    gain_first = fetch(gain_in).astype(SINGLE)
    gain_second = fetch(gain_mid).astype(SINGLE)
    projections = [fetch(w) for w in (w_query, w_key, w_value, w_house)]
    mat_rate = fetch(w_rate)
    tap_values = fetch(conv_taps, 1).astype(SINGLE)
    mat_out, mat_gate, mat_up, mat_down = [fetch(w) for w in (w_out, w_gate, w_up, w_down)]
    turn, marks, segc, segr = turned(doc_ids[0], conv_taps.shape[0])
    rows = mm(turn, tokens[0])
    upstream = mm(turn, cotangent[0]).astype(HALF)
    unit_in, inverse_in = unit_norm(rows)
    normed = (unit_in * gain_first).astype(HALF)
    rate_sig = jax.nn.sigmoid(
        lax.dot_general(mat_rate, normed, (((0,), (1,)), ((), ())), preferred_element_type=SINGLE)
    )
    rates = [2.0 * rate_sig[k * count : (k + 1) * count] for k in range(4)]
    taps = [tap_values[:, k * wide : (k + 1) * wide] for k in range(4)]
    pieces = [
        jnp.concatenate([w[:, k * wide : (k + 1) * wide] for w in projections], axis=1) for k in range(4)
    ]
    kept = [
        attn_forward(normed, [pieces[k]], rates[k], taps[k], marks, segc, segr, dim, span) for k in range(4)
    ]
    attended = jnp.concatenate([k[0] for k in kept], axis=1)
    middle = rows + mm(attended, mat_out)
    unit_mid, inverse_mid = unit_norm(middle)
    normed_mid = (unit_mid * gain_second).astype(HALF)
    gate_rows = mm(normed_mid, mat_gate)
    up_rows = mm(normed_mid, mat_up)
    gate_sig, hidden = gates(gate_rows, up_rows)
    result = (middle + mm(hidden, mat_down)).astype(HALF)
    feed_rows = gates_back(mm_nt(upstream, mat_down), gate_rows, up_rows, gate_sig)
    units = feed_rows.shape[1] // 2
    grad_gate_rows, grad_up_rows = feed_rows[:, :units], feed_rows[:, units:]
    grad_normed_mid = mm_nt(grad_gate_rows, mat_gate) + mm_nt(grad_up_rows, mat_up)
    grad_middle = upstream.astype(SINGLE) + unit_back(grad_normed_mid, unit_mid, inverse_mid, gain_second)
    grad_branch = grad_middle.astype(HALF)
    grad_att = mm_nt(grad_branch, mat_out).astype(HALF)
    row_grads, rate_grads, tap_grads = [], [], []
    for k in range(4):
        unused_out, qkv, raw, house, tri, carried, probs = kept[k]
        got = attn_backward(
            qkv, house, raw, rates[k], taps[k], marks, segc, segr, grad_att[None, :, k * wide : (k + 1) * wide], 0,
            tri, carried, probs, dim, span,
        )
        row_grads.append(got[0])
        rate_grads.append(got[1])
        tap_grads.append(got[2])
    grad_rate_rows = (jnp.concatenate(rate_grads, axis=0) * 2.0 * rate_sig * (1.0 - rate_sig)).astype(HALF)
    grad_normed = lax.dot_general(
        grad_rate_rows, mat_rate, (((0,), (1,)), ((), ())), preferred_element_type=SINGLE
    )
    for k in range(4):
        grad_normed = grad_normed + mm_nt(row_grads[k], pieces[k])
    grad_tokens = grad_middle + unit_back(grad_normed, unit_in, inverse_in, gain_first)
    weight_grads = []
    for m in range(4):
        part = jnp.concatenate([r[:, m * wide : (m + 1) * wide] for r in row_grads], axis=1)
        weight_grads.append(share(mm_tn(normed, part)))
    return (
        mm_tn(turn, result).astype(HALF)[None],
        turn_back(turn, grad_tokens)[None],
        share(jnp.sum(grad_normed * unit_in, axis=0)),
        weight_grads[0],
        weight_grads[1],
        weight_grads[2],
        weight_grads[3],
        share(lax.dot_general(normed, grad_rate_rows, (((0,), (1,)), ((), ())), preferred_element_type=SINGLE)),
        share(jnp.concatenate(tap_grads, axis=1), 1),
        share(mm_tn(attended, grad_branch)),
        share(jnp.sum(grad_normed_mid * unit_mid, axis=0)),
        share(mm_tn(normed_mid, grad_gate_rows)),
        share(mm_tn(normed_mid, grad_up_rows)),
        share(mm_tn(hidden, upstream)),
    )


class Links:
    def __init__(self, groups, shards):
        self.core = lax.axis_index("grp") % 2
        self.me = lax.axis_index("fsdp")
        near = 1 + self.core
        self.order = [self.me, self.me ^ near, self.me ^ (3 - near), self.me ^ 3]

        def permutation(move):
            pairs = []
            for g in range(groups):
                for f in range(shards):
                    target = move(g // 2, g % 2, f)
                    if target is not None:
                        pairs.append((g * shards + f, target[0] * shards + target[1]))
            return pairs

        self.pairs = {
            "near": permutation(lambda z, c, f: (2 * z + c, f ^ (1 + c))),
            "next": permutation(lambda z, c, f: (2 * z + c, f ^ (2 - c))),
            "twin": permutation(lambda z, c, f: (2 * z + 1 - c, f)),
            "far": permutation(lambda z, c, f: (2 * z + c, f ^ 3)),
            "level": permutation(lambda z, c, f: (2 * (z ^ 1) + c, f)),
            "pair": permutation(lambda z, c, f: (2 * (3 - z) + c, f)),
            "inward": permutation(lambda z, c, f: (2 * (z ^ 1) + c, f) if z in (0, 3) else None),
            "across": permutation(lambda z, c, f: (2 * (3 - z) + c, f) if z in (1, 2) else None),
            "outward": permutation(lambda z, c, f: (2 * (z ^ 1) + c, f) if z in (1, 2) else None),
        }
        level = lax.axis_index("grp") // 2
        self.edge = (level == 0) | (level == 3)
        self.keep = jnp.where(self.edge, 0, 1)
        self.columns = [[2 * z + c for z in range(groups // 2)] for c in range(2)]

    def near(self, array):
        return lax.ppermute(array, AXES, self.pairs["near"])

    def next(self, array):
        return lax.ppermute(array, AXES, self.pairs["next"])

    def twin(self, array):
        return lax.ppermute(array, AXES, self.pairs["twin"])

    def far(self, array):
        return lax.ppermute(array, AXES, self.pairs["far"])

    def level(self, array):
        return lax.ppermute(array, AXES, self.pairs["level"])

    def pair(self, array):
        return lax.ppermute(array, AXES, self.pairs["pair"])

    def inward(self, array):
        return lax.ppermute(array, AXES, self.pairs["inward"])

    def across(self, array):
        return lax.ppermute(array, AXES, self.pairs["across"])

    def outward(self, array):
        return lax.ppermute(array, AXES, self.pairs["outward"])

    def settled(self, total, got):
        return jnp.where(self.edge, got, total)

    def halves(self, array, axis):
        pick = lambda i: lax.dynamic_index_in_dim(array, i, axis, keepdims=False)
        return pick(self.keep), pick(1 - self.keep)

    def joined(self, mine, partner, axis):
        return jnp.where(
            self.edge, jnp.stack([mine, partner], axis=axis), jnp.stack([partner, mine], axis=axis)
        )

    def place(self, number):
        apart = number ^ self.me
        return jnp.where((apart == 0) | (apart == 3) | (self.core == 0), apart, 3 - apart)

    def in_place(self, blocks):
        rows = blocks[0].shape[0]
        every = jnp.zeros((rows * 4,) + blocks[0].shape[1:], blocks[0].dtype)
        for number, block in zip(self.order, blocks):
            every = lax.dynamic_update_slice(every, block, (number * rows,) + (0,) * (block.ndim - 1))
        return every

    def by_core(self, own, other, axis):
        return jnp.where(
            self.core == 0,
            jnp.concatenate([own, other], axis=axis),
            jnp.concatenate([other, own], axis=axis),
        )


def core_sum(own, got):
    rows = own.shape[0] // 4
    flip = [got[i * rows : (i + 1) * rows] for i in (0, 2, 1, 3)]
    head = wide_sum(own[: 2 * rows], jnp.concatenate(flip[:2], axis=0)).astype(HALF)
    tail = wide_sum(own[2 * rows :], jnp.concatenate(flip[2:], axis=0)).astype(HALF)
    return head, tail


def second_sum(head, got):
    rows = head.shape[0] // 2
    return wide_sum(head[:rows], got[:rows]), wide_sum(head[rows:], got[rows:]).astype(HALF)


def local_paired(
    tokens, doc_ids, cotangent, gain_in, w_query, w_key, w_value, w_house, w_rate, conv_taps, w_out,
    gain_mid, w_gate, w_up, w_down, *, groups, shards,
):
    links = Links(groups, shards)
    core = links.core
    length = tokens.shape[1]
    width = tokens.shape[2]
    span = length // 2
    heads = w_rate.shape[1]
    dim = width // heads
    taps_count = conv_taps.shape[0]
    part = width // shards
    half_width = width // 2
    count = heads // 4
    wide = count * dim
    own_at = core * half_width
    other_at = half_width - own_at
    number = [2 * core, 2 * core + 1, 2 - 2 * core, 3 - 2 * core]
    hidden_part = w_gate.shape[1] // shards
    h = hidden_part // 2
    hid_own = core * h
    hid_other = h - hid_own

    def group_columns(k):
        return jnp.concatenate(
            [cut(matrix, k * wide, wide, 1).astype(HALF) for matrix in (w_query, w_key, w_value, w_house)],
            axis=1,
        )

    def feed_block(i):
        start = i * hidden_part + hid_own
        return jnp.concatenate([cut(w_gate, start, h, 1), cut(w_up, start, h, 1)], axis=1).astype(HALF)

    def in_order(array, axis):
        return jnp.concatenate([cut(array, i * part, part, axis) for i in links.order], axis=axis)

    def from_order(array, axis):
        return jnp.concatenate([cut(array, links.place(i) * part, part, axis) for i in range(4)], axis=axis)

    small = jnp.concatenate([gain_in[:, None], gain_mid[:, None], conv_taps.T, w_rate], axis=1).astype(HALF)
    small = jnp.pad(small, ((0, 0), (0, 128 - small.shape[1])))
    small_near, small_second, small_far = links.near(small), links.next(small), links.far(small)
    block0 = group_columns(number[0])
    near0, second0 = links.near(block0), links.next(block0)

    turn, marks, segc, segr = turned(doc_ids[0], taps_count)
    rows = mm(turn, tokens[0])
    unit_in, inverse_in = unit_norm(rows)
    unit_in = in_order(unit_in, 1)
    block1 = group_columns(number[1])

    near0, second0, small_near, small_second, small_far, block1, unit_in = tie(
        near0, second0, small_near, small_second, small_far, block1, unit_in
    )
    far0 = links.next(near0)
    twin0 = [links.twin(second0), links.twin(near0)]
    small = [small, small_near, small_second, small_far]
    small_order = jnp.concatenate(small, axis=0)
    small_plain = links.in_place(small)
    gain_first = small_order[:, 0].astype(SINGLE)
    gain_second = small_plain[:, 1].astype(SINGLE)
    tap_values = small_plain[:, 2 : 2 + taps_count].astype(SINGLE)
    mat_rate = small_order[:, 2 + taps_count : 2 + taps_count + heads]
    normed = (unit_in * gain_first).astype(HALF)
    rate_sig = jax.nn.sigmoid(
        lax.dot_general(mat_rate, normed, (((0,), (1,)), ((), ())), preferred_element_type=SINGLE)
    )
    rates = [cut(2.0 * rate_sig, k * count, count, 0) for k in number]
    taps = [cut(tap_values, k * wide, wide, 0).T for k in number]
    normed, far0, block1, *rest = tie(normed, far0, block1, *rates, *taps)
    rates, taps = rest[:4], rest[4:]

    def forward(i, normed, pieces):
        return attn_forward(normed, pieces, rates[i], taps[i], marks, segc, segr, dim, span)

    kept = [None] * 4
    pieces = [None] * 4
    pieces[0] = [block0, near0, second0, far0]
    twin0.append(links.twin(far0))
    near1, second1 = links.near(block1), links.next(block1)
    kept[0] = forward(0, normed, pieces[0])
    block2 = group_columns(number[2])
    out_block = cut(w_out, own_at, half_width, 1).astype(HALF)

    normed, unused, near1, second1, out_block, block2, *twin0 = tie(
        normed, kept[0][0], near1, second1, out_block, block2, *twin0
    )
    far1 = links.next(near1)
    twin1 = [links.twin(second1), links.twin(near1)]
    pieces[2] = [block2] + twin0
    kept[2] = forward(2, normed, pieces[2])
    block3 = group_columns(number[3])
    out_rest = cut(w_out, other_at, half_width, 1).astype(HALF)

    far1, normed, unused, out_block, block3, out_rest = tie(far1, normed, kept[2][0], out_block, block3, out_rest)
    twin1.append(links.twin(far1))
    pieces[1] = [block1, near1, second1, far1]
    out_near, out_second = links.near(out_block), links.next(out_block)
    kept[1] = forward(1, normed, pieces[1])
    feed_first, feed_second, feed_far = [feed_block(i) for i in links.order[1:]]
    upstream = mm(turn, cotangent[0]).astype(HALF)

    normed, unused, out_near, out_second, feed_first, feed_second, feed_far, upstream, *twin1 = tie(
        normed, kept[1][0], out_near, out_second, feed_first, feed_second, feed_far, upstream, *twin1
    )
    pieces[3] = [block3] + twin1
    out_far = links.next(out_near)
    feed_passing = links.near(feed_far)
    feed_near = links.near(feed_first)
    feed_next = links.next(feed_second)
    out_twin = [links.twin(out_second), links.twin(out_near)]
    kept[3] = forward(3, normed, pieces[3])

    att3, out_far, feed_passing, *out_twin = tie(kept[3][0], out_far, feed_passing, *out_twin)
    feed_last = links.next(feed_passing)
    up_near, up_second = links.near(upstream), links.next(upstream)
    out_twin.append(links.twin(out_far))
    places = [links.place(k) for k in number] + [own_at] + [k ^ (2 * core) for k in links.order]
    places = jnp.stack([jnp.asarray(p, jnp.int32) for p in places])
    gain_second = gain_second[None, :]
    out_own = [out_block, out_near, out_second, out_far]
    out_other = [out_rest] + out_twin
    attended, middle, normed_mid = leave_attention(
        places, rows, gain_second, [kept[0][0], kept[1][0], kept[2][0], att3], out_own, out_other
    )

    normed_mid, feed_near, feed_next, up_near, up_second = tie(
        normed_mid, feed_near, feed_next, up_near, up_second
    )

    mid_near, mid_second = links.near(normed_mid), links.next(normed_mid)
    feed_mine = feed_block(links.me)
    mat_down = jnp.concatenate(
        [cut(w_down, hid_own, h, 0), cut(w_down, hid_other, h, 0)], axis=0
    ).astype(HALF)
    mid_near, mid_second, feed_mine, mat_down = tie(mid_near, mid_second, feed_mine, mat_down)
    mid_far = links.next(mid_near)
    feed_own = links.in_place([feed_mine, feed_near, feed_next, feed_last])
    feed_other = links.twin(feed_own)
    mat_feed = jnp.concatenate(
        [feed_own[:, :h], feed_other[:, :h], feed_own[:, h:], feed_other[:, h:]], axis=1
    )
    mat_feed, mid_far, up_near = tie(mat_feed, mid_far, up_near)
    up_far = links.next(up_near)
    normed_all = jnp.concatenate([normed_mid, mid_near, mid_second, mid_far], axis=0)
    gate_up, hidden, down_part = feed_forward(normed_all, mat_feed, mat_down, shards)
    up_far, gate_up, hidden = tie(up_far, gate_up, hidden)
    upstream_all = jnp.concatenate([upstream, up_near, up_second, up_far], axis=0)
    feed_rows, mid_tail = feed_backward(upstream_all, gate_up, mat_feed, mat_down, shards, 2, 2)

    mid_tail, feed_rows, hidden, upstream_all = tie(mid_tail, feed_rows, hidden, upstream_all)
    mid_got = links.next(mid_tail)
    grad_down = mm_tn(hidden, upstream_all).astype(HALF)
    grad_down, feed_rows, upstream_all = tie(grad_down, feed_rows, upstream_all)
    down_got = links.twin(grad_down[h:])
    feed_rows, mid_head = feed_backward(upstream_all, gate_up, mat_feed, mat_down, shards, 0, 2, feed_rows)
    mid_got, mid_head, down_got, feed_rows = tie(mid_got, mid_head, down_got, feed_rows)
    mid_own, mid_first = second_sum(mid_head, mid_got)
    mid_last = links.near(mid_first)
    down_sum = wide_sum(grad_down[:h], down_got).astype(HALF)
    down_in = links.inward(down_sum)
    grad_feed = mm_tn(normed_all, feed_rows).astype(HALF)

    mid_last, grad_feed, mid_own, down_part = tie(mid_last, grad_feed, mid_own, down_part)
    feed_got = links.twin(jnp.concatenate([grad_feed[:, h : 2 * h], grad_feed[:, 3 * h :]], axis=1))
    result_got = links.next(down_part[2 * length :])
    grad_middle, branch_pair, grad_gain_mid, grad_att = return_to_attention(
        places, mid_own, mid_last, upstream, middle, gain_second, out_own, out_other
    )
    out_grads = mm_tn(attended, branch_pair).astype(HALF)

    def backward(i, grad_att):
        unused_out, qkv, raw, house, tri, carried, probs = kept[i]
        return attn_backward(
            qkv, house, raw, rates[i], taps[i], marks, segc, segr, grad_att, i, tri, carried, probs, dim, span
        )

    row_grads = [None] * 4
    rate_grads = [None] * 4
    tap_grads = [None] * 4
    out_grads, feed_got, grad_att = tie(out_grads, feed_got, grad_att)
    out_got = links.twin(out_grads[:, half_width:])
    feed_sum = wide_sum(
        jnp.concatenate([grad_feed[:, :h], grad_feed[:, 2 * h : 3 * h]], axis=1), feed_got
    ).astype(HALF)
    feed0, feed1 = feed_sum[: width // 2], feed_sum[width // 2 :]
    row_grads[2], rate_grads[2], tap_grads[2] = backward(2, grad_att)
    other = mm_tn(normed, row_grads[2]).astype(HALF)

    other, out_got, grad_att, down_in, feed0, feed1, result_got = tie(
        other, out_got, grad_att, down_in, feed0, feed1, result_got
    )
    got0 = links.twin(other)
    feed0_in = links.inward(feed0)
    down_sum = wide_sum(down_sum, down_in).astype(HALF)
    down_across = links.across(down_sum)
    out_head, out_tail = core_sum(out_grads[:, :half_width], out_got)
    out_part = links.next(out_tail)
    result_own, result_first = second_sum(down_part[: 2 * length], result_got)
    result_last = links.near(result_first)
    row_grads[0], rate_grads[0], tap_grads[0] = backward(0, grad_att)
    own0 = mm_tn(normed, row_grads[0]).astype(HALF)

    own0, got0, out_part, grad_att = tie(own0, got0, out_part, grad_att)
    head0, tail0 = core_sum(own0, got0)
    part0 = links.next(tail0)
    out_own_sum, out_first = second_sum(out_head, out_part)
    out_last = links.near(out_first)
    row_grads[3], rate_grads[3], tap_grads[3] = backward(3, grad_att)
    other = mm_tn(normed, row_grads[3]).astype(HALF)

    other, out_last, grad_att, feed0_in, down_across, result_last = tie(
        other, out_last, grad_att, feed0_in, down_across, result_last
    )
    got1 = links.twin(other)
    feed1_in = links.inward(feed1)
    feed0 = wide_sum(feed0, feed0_in).astype(HALF)
    feed0_across = links.across(feed0)
    down_sum = wide_sum(down_sum, down_across).astype(HALF)
    down_out = links.outward(down_sum)
    out_sum = wide_sum(out_own_sum, out_last).astype(HALF)
    result = (middle + wide_sum(result_own, result_last)).astype(HALF)
    result = mm_tn(turn, result).astype(HALF)
    row_grads[1], rate_grads[1], tap_grads[1] = backward(1, grad_att)
    own1 = mm_tn(normed, row_grads[1]).astype(HALF)

    own1, got1, part0, out_sum, feed1_in, feed0_across, *late = tie(
        own1, got1, part0, out_sum, feed1_in, feed0_across, *row_grads
    )
    feed1 = wide_sum(feed1, feed1_in).astype(HALF)
    feed1_across = links.across(feed1)
    feed0 = wide_sum(feed0, feed0_across).astype(HALF)
    feed0_out = links.outward(feed0)
    sum0, first0 = second_sum(head0, part0)
    last0 = links.near(first0)
    head1, tail1 = core_sum(own1, got1)
    part1 = links.next(tail1)

    grad_rate = links.by_core(
        jnp.concatenate(rate_grads[:2], axis=0), jnp.concatenate(rate_grads[2:], axis=0), 0
    )
    grad_taps = links.by_core(
        jnp.concatenate(tap_grads[:2], axis=1), jnp.concatenate(tap_grads[2:], axis=1), 1
    )
    grad_rate_rows = (grad_rate * 2.0 * rate_sig * (1.0 - rate_sig)).astype(HALF)
    grad_wrate = lax.dot_general(
        normed, grad_rate_rows, (((0,), (1,)), ((), ())), preferred_element_type=SINGLE
    )
    grad_normed = lax.dot_general(
        grad_rate_rows, mat_rate, (((0,), (1,)), ((), ())), preferred_element_type=SINGLE
    )
    for i in (0, 2):
        grad_normed = grad_normed + mm_nt(late[i], jnp.concatenate(pieces[i], axis=0))

    last0, grad_normed, down_out, feed1_across = tie(last0, grad_normed, down_out, feed1_across)
    feed1 = wide_sum(feed1, feed1_across).astype(HALF)
    feed1_out = links.outward(feed1)
    out_in = links.inward(out_sum)
    sum0 = wide_sum(sum0, last0).astype(HALF)
    sum0_in = links.inward(sum0)
    down_sum = links.settled(down_sum, down_out)
    down_twin = links.twin(down_sum)
    for i in (1, 3):
        grad_normed = grad_normed + mm_nt(late[i], jnp.concatenate(pieces[i], axis=0))
    grad_gain_in = jnp.sum(grad_normed * unit_in, axis=0)
    extra = jnp.concatenate(
        [grad_gain_in[:, None], in_order(grad_gain_mid[0], 0)[:, None], in_order(grad_taps.T, 0), grad_wrate],
        axis=1,
    )
    extra = jnp.pad(extra, ((0, 0), (0, 128 - extra.shape[1]))).astype(HALF)

    extra, part1, out_in, grad_normed = tie(extra, part1, out_in, grad_normed)
    extra_got = links.twin(extra)
    sum1, first1 = second_sum(head1, part1)
    last1 = links.near(first1)
    out_sum = wide_sum(out_sum, out_in).astype(HALF)
    out_across = links.across(out_sum)
    norm_grad = unit_back(grad_normed, unit_in, inverse_in, gain_first)
    grad_tokens = turn_back(turn, grad_middle + from_order(norm_grad, 1))

    grad_tokens, sum0_in, extra_got, last1, feed0_out = tie(
        grad_tokens, sum0_in, extra_got, last1, feed0_out
    )
    sum0 = wide_sum(sum0, sum0_in).astype(HALF)
    sum0_across = links.across(sum0)
    sum1 = wide_sum(sum1, last1).astype(HALF)
    sum1 = [sum1[: part // 2], sum1[part // 2 :]]
    sum1_in = [links.inward(a) for a in sum1]
    extra_head, extra_tail = core_sum(extra, extra_got)
    extra_part = links.next(extra_tail)
    grad_down = links.by_core(down_sum, down_twin, 0).astype(SINGLE)
    feed0 = links.settled(feed0, feed0_out)

    feed1_out, sum0_across, out_across, extra_part, grad_down, feed0, *sum1_in = tie(
        feed1_out, sum0_across, out_across, extra_part, grad_down, feed0, *sum1_in
    )
    sum0 = wide_sum(sum0, sum0_across).astype(HALF)
    sum0_out = links.outward(sum0)
    sum1 = [wide_sum(a, b).astype(HALF) for a, b in zip(sum1, sum1_in)]
    sum1_across = [links.across(a) for a in sum1]
    out_sum = wide_sum(out_sum, out_across).astype(HALF)
    out_out = links.outward(out_sum)
    feed_sum = jnp.concatenate([feed0, links.settled(feed1, feed1_out)], axis=0)
    feed_blocks = [cut(feed_sum, i * part, part, 0) for i in links.order]
    feed_passing, feed_near = links.near(feed_blocks[3]), links.near(feed_blocks[1])
    feed_next = links.next(feed_blocks[2])
    extra_own, extra_first = second_sum(extra_head, extra_part)
    extra_last = links.near(extra_first)

    feed_passing, extra_last, *sum1_across = tie(feed_passing, extra_last, *sum1_across)
    feed_last = links.next(feed_passing)
    sum1 = [wide_sum(a, b).astype(HALF) for a, b in zip(sum1, sum1_across)]
    sum1_out = [links.outward(a) for a in sum1]
    extra_sum = wide_sum(extra_own, extra_last).astype(HALF)
    extra_level = links.level(extra_sum)

    feed_last, sum0_out, out_out, extra_level, *sum1_out = tie(
        feed_last, sum0_out, out_out, extra_level, *sum1_out
    )
    out_sum = links.settled(out_sum, out_out)
    out_twin = links.twin(out_sum)
    sum0 = links.settled(sum0, sum0_out)
    twin0 = links.twin(sum0)
    extra_sum = wide_sum(extra_sum, extra_level).astype(HALF)
    extra_pair = links.pair(extra_sum)
    grad_wout = links.by_core(out_sum, out_twin, 1).astype(SINGLE)

    feed_mine = links.in_place([feed_blocks[0], feed_near, feed_next, feed_last])
    feed_twin = links.twin(feed_mine)
    sum1 = jnp.concatenate([links.settled(a, b) for a, b in zip(sum1, sum1_out)], axis=0)
    twin1 = links.twin(sum1)
    extra = wide_sum(extra_sum, extra_pair)

    grad_gate, grad_up = [
        jnp.concatenate(
            [
                links.by_core(
                    feed_mine[i * part : (i + 1) * part, at : at + h],
                    feed_twin[i * part : (i + 1) * part, at : at + h],
                    1,
                )
                for i in range(shards)
            ],
            axis=1,
        ).astype(SINGLE)
        for at in (0, h)
    ]
    sums = [(sum0, twin0), (sum1, twin1)]
    weight_grads = []
    for m in range(4):
        columns = [[a[:, m * wide : (m + 1) * wide] for a in pair] for pair in sums]
        weight_grads.append(
            links.by_core(
                jnp.concatenate([columns[0][0], columns[1][0]], axis=1),
                jnp.concatenate([columns[0][1], columns[1][1]], axis=1),
                1,
            ).astype(SINGLE)
        )

    return (
        result[None],
        grad_tokens[None],
        extra[:, 0],
        weight_grads[0],
        weight_grads[1],
        weight_grads[2],
        weight_grads[3],
        extra[:, 2 + taps_count : 2 + taps_count + heads],
        extra[:, 2 : 2 + taps_count].T,
        grad_wout,
        extra[:, 1],
        grad_gate,
        grad_up,
        grad_down,
    )


def solution(mesh):
    groups, shards = mesh.shape["grp"], mesh.shape["fsdp"]
    if (groups, shards) == (8, 4):
        body = functools.partial(local_paired, groups=groups, shards=shards)
    else:
        body = local_any
    rows = P(("grp", "fsdp"), None, None)
    vector = P("fsdp")
    matrix = P("fsdp", None)
    taps = P(None, "fsdp")
    return jax.shard_map(
        body,
        mesh=mesh,
        in_specs=(
            rows, P(("grp", "fsdp"), None), rows, vector, matrix, matrix, matrix, matrix, matrix,
            taps, matrix, vector, matrix, matrix, matrix,
        ),
        out_specs=(
            rows, rows, vector, matrix, matrix, matrix, matrix, matrix, taps, matrix, vector,
            matrix, matrix, matrix,
        ),
        check_vma=False,
    )
```

```python
import functools
import jax
import jax.numpy as jnp
from jax import lax
from jax.experimental import pallas as pl
from jax.experimental.pallas import tpu as pltpu
from jax.sharding import PartitionSpec as P

EPS = 1e-06
HALF = jnp.bfloat16
SINGLE = jnp.float32


def mm(left, right):
    return lax.dot_general(left, right, (((1,), (0,)), ((), ())), preferred_element_type=SINGLE)


def mm_nt(left, right):
    return lax.dot_general(left, right, (((1,), (1,)), ((), ())), preferred_element_type=SINGLE)


def mm_tn(left, right):
    return lax.dot_general(left, right, (((0,), (0,)), ((), ())), preferred_element_type=SINGLE)


def conv_parts(raw, taps, marks, taps_count):
    shifted = [raw]
    total = raw * taps[0:1, :]
    for k in range(1, taps_count):
        moved = pltpu.roll(raw, k, 0) * marks[:, k : k + 1]
        shifted.append(moved)
        total = total + moved * taps[k : k + 1, :]
    return shifted, total


def attn_forward_kernel(
    span, dim, count, taps_count, number, *refs
):
    normed_ref = refs[0]
    piece_refs = refs[1 : 1 + number]
    rate_ref, taps_ref, marks_ref, segc_ref, segr_ref = refs[1 + number : 6 + number]
    out_ref, qkv_ref, raw_ref, w_ref, t_ref, c_ref, p_ref = refs[6 + number :]
    blocks = normed_ref.shape[0] // span
    wide = count * dim
    depth = normed_ref.shape[1] // number
    for m in (3, 0, 1, 2):
        total = mm(normed_ref[:, :depth], piece_refs[0][:, m * wide : (m + 1) * wide])
        for r in range(1, number):
            total = total + mm(
                normed_ref[:, r * depth : (r + 1) * depth], piece_refs[r][:, m * wide : (m + 1) * wide]
            )
        if m == 3:
            raw_ref[...] = total
        else:
            qkv_ref[:, m * wide : (m + 1) * wide] = total.astype(HALF)
    q_ref, k_ref, v_ref = [qkv_ref.at[:, m * wide : (m + 1) * wide] for m in range(3)]
    marks = marks_ref[...]
    row_id = lax.broadcasted_iota(jnp.int32, (span, span), 0)
    col_id = lax.broadcasted_iota(jnp.int32, (span, span), 1)
    eye = jnp.where(row_id == col_id, 1.0, 0.0)
    sizes = []
    size = 1
    while size < span:
        sizes.append(size)
        size *= 2
    level_of = {}
    for size in sizes:
        level_of[size] = ((row_id // (2 * size)) == (col_id // (2 * size))) & (
            (row_id // size) > (col_id // size)
        )
    strict = []
    inclusive = []
    for u in range(blocks):
        rows = slice(u * span, (u + 1) * span)
        same = segc_ref[rows, 0:1] == segr_ref[0:1, rows]
        strict.append(same & (col_id < row_id))
        inclusive.append(same & (col_id <= row_id))
    for h in range(count):
        cols = slice(h * dim, (h + 1) * dim)
        shifted, mixed = conv_parts(raw_ref[:, cols], taps_ref[:, cols], marks, taps_count)
        inverse = lax.rsqrt(jnp.sum(mixed * mixed, axis=-1, keepdims=True) + EPS)
        w_ref[:, cols] = (mixed * inverse).astype(HALF)
    units = [(h, u) for h in range(count) for u in range(blocks)]
    rates = {}
    lower = {}
    inv = {}
    for h, u in units:
        rows = slice(u * span, (u + 1) * span)
        cols = slice(h * dim, (h + 1) * dim)
        w = w_ref[rows, cols]
        rates[h, u] = rate_ref[h : h + 1, rows]
        lw = jnp.where(strict[u], mm_nt(w, w) * rates[h, u], 0.0)
        lower[h, u] = lw.astype(HALF)
        inv[h, u] = eye - jnp.where(level_of[1], lw, 0.0)
    for size in sizes[1:]:
        half_inv = {}
        inner = {}
        for unit in units:
            half_inv[unit] = inv[unit].astype(HALF)
            inner[unit] = mm(jnp.where(level_of[size], lower[unit], jnp.zeros_like(lower[unit])), half_inv[unit])
        for unit in units:
            inv[unit] = inv[unit] - mm(half_inv[unit], inner[unit].astype(HALF))
    for h, u in units:
        rows = slice(u * span, (u + 1) * span)
        cols = slice(h * dim, (h + 1) * dim)
        w = w_ref[rows, cols]
        q = q_ref[rows, cols]
        k = k_ref[rows, cols]
        tri = inv[h, u].astype(HALF)
        t_ref[h * blocks + u] = tri
        right = jnp.where(strict[u], mm_nt(w, k), 0.0).astype(HALF)
        carried = mm(tri, right).astype(HALF)
        c_ref[h * blocks + u] = carried
        reach = (jnp.where(inclusive[u], mm_nt(q, w), 0.0) * rates[h, u]).astype(HALF)
        scores = (mm_nt(q, k) - mm(reach, carried)) * dim ** (-0.5)
        scores = jnp.where(inclusive[u], scores, -1e30)
        terms = jnp.exp(scores - jnp.max(scores, axis=1, keepdims=True))
        probs = (terms / jnp.sum(terms, axis=1, keepdims=True)).astype(HALF)
        p_ref[h * blocks + u] = probs
        out_ref[rows, cols] = mm(probs, v_ref[rows, cols]).astype(HALF)


def attn_backward_kernel(
    span, dim, count, taps_count,
    qkv_ref, w_ref, raw_ref, rate_ref, taps_ref, marks_ref, segc_ref, segr_ref, grad_ref, t_ref, c_ref, p_ref,
    out_ref, drate_ref, dtaps_ref, dw_ref,
):
    blocks = qkv_ref.shape[0] // span
    wide = count * dim
    q_ref, k_ref, v_ref = [qkv_ref.at[:, m * wide : (m + 1) * wide] for m in range(3)]
    dq_ref, dk_ref, dv_ref, draw_ref = [out_ref.at[:, m * wide : (m + 1) * wide] for m in range(4)]
    marks = marks_ref[...]
    row_id = lax.broadcasted_iota(jnp.int32, (span, span), 0)
    col_id = lax.broadcasted_iota(jnp.int32, (span, span), 1)
    scale = dim ** (-0.5)
    for u in range(blocks):
        rows = slice(u * span, (u + 1) * span)
        same = segc_ref[rows, 0:1] == segr_ref[0:1, rows]
        strict = same & (col_id < row_id)
        inclusive = same & (col_id <= row_id)
        for h in range(count):
            cols = slice(h * dim, (h + 1) * dim)
            unit = h * blocks + u
            q = q_ref[rows, cols]
            k = k_ref[rows, cols]
            v = v_ref[rows, cols]
            w = w_ref[rows, cols]
            grad = grad_ref[0, rows, cols]
            rate = rate_ref[h : h + 1, rows]
            probs = p_ref[unit]
            carried = c_ref[unit]
            tri = t_ref[unit]
            dprobs = mm_nt(grad, v)
            dv_ref[rows, cols] = mm_tn(probs, grad).astype(HALF)
            probs = probs.astype(SINGLE)
            weighted = probs * dprobs
            dscore = ((weighted - probs * jnp.sum(weighted, axis=1, keepdims=True)) * scale).astype(HALF)
            reach_raw = jnp.where(inclusive, mm_nt(q, w), 0.0)
            reach = (reach_raw * rate).astype(HALF)
            dreach = -mm_nt(dscore, carried)
            drate = jnp.sum(dreach * reach_raw, axis=0, keepdims=True)
            dreach = (jnp.where(inclusive, dreach, 0.0) * rate).astype(HALF)
            dcarried = (-mm_tn(reach, dscore)).astype(HALF)
            dright = jnp.where(strict, mm_tn(tri, dcarried), 0.0).astype(HALF)
            dlower = jnp.where(strict, -mm_nt(dright, carried), 0.0)
            drate = drate + jnp.sum(dlower * mm_nt(w, w), axis=0, keepdims=True)
            dlower = (dlower * rate).astype(HALF)
            dq_ref[rows, cols] = (mm(dscore, k) + mm(dreach, w)).astype(HALF)
            dk_ref[rows, cols] = (mm_tn(dscore, q) + mm_tn(dright, w)).astype(HALF)
            dw_ref[rows, cols] = mm_tn(dreach, q) + mm(dright, k) + mm(dlower, w) + mm_tn(dlower, w)
            drate_ref[h : h + 1, rows] = drate
    length = q_ref.shape[0]
    for h in range(count):
        cols = slice(h * dim, (h + 1) * dim)
        taps = taps_ref[:, cols]
        shifted, mixed = conv_parts(raw_ref[:, cols], taps, marks, taps_count)
        inverse = lax.rsqrt(jnp.sum(mixed * mixed, axis=-1, keepdims=True) + EPS)
        unit_rows = mixed * inverse
        dw = dw_ref[:, cols]
        dmixed = inverse * (dw - unit_rows * jnp.sum(dw * unit_rows, axis=-1, keepdims=True))
        draw = dmixed * taps[0:1, :]
        dtaps = [jnp.sum(dmixed * shifted[0], axis=0, keepdims=True)]
        for k in range(1, taps_count):
            dtaps.append(jnp.sum(dmixed * shifted[k], axis=0, keepdims=True))
            draw = draw + pltpu.roll(dmixed * marks[:, k : k + 1], length - k, 0) * taps[k : k + 1, :]
        draw_ref[:, cols] = draw.astype(HALF)
        dtaps_ref[:, cols] = jnp.concatenate(dtaps, axis=0)


def attn_forward(normed, pieces, rate, taps, marks, segc, segr, dim, span):
    length = normed.shape[0]
    count = rate.shape[0]
    wide = count * dim
    units = count * (length // span)
    square = jax.ShapeDtypeStruct((units, span, span), HALF)
    return pl.pallas_call(
        functools.partial(attn_forward_kernel, span, dim, count, taps.shape[0], len(pieces)),
        out_shape=[
            jax.ShapeDtypeStruct((length, wide), HALF),
            jax.ShapeDtypeStruct((length, 3 * wide), HALF),
            jax.ShapeDtypeStruct((length, wide), SINGLE),
            jax.ShapeDtypeStruct((length, wide), HALF),
            square, square, square,
        ],
        compiler_params=pltpu.CompilerParams(vmem_limit_bytes=60 * 1024 * 1024),
        cost_estimate=pl.CostEstimate(flops=16000000000, bytes_accessed=12000000, transcendentals=0),
        name="attend",
    )(normed, *pieces, rate, taps, marks, segc, segr)


def attn_backward(qkv, w, raw, rate, taps, marks, segc, segr, grads, group, tri, carried, probs, dim, span):
    length = qkv.shape[0]
    count = rate.shape[0]
    wide = count * dim
    whole = lambda a: pl.BlockSpec(a.shape, lambda g: (0,) * a.ndim)
    small = lambda shape: pl.BlockSpec(shape, lambda g: (0, 0))
    return pl.pallas_call(
        functools.partial(attn_backward_kernel, span, dim, count, taps.shape[0]),
        grid=(1,),
        in_specs=[whole(a) for a in (qkv, w, raw, rate, taps, marks, segc, segr)]
        + [pl.BlockSpec((1, length, wide), lambda g: (group, 0, 0))]
        + [whole(a) for a in (tri, carried, probs)],
        out_specs=[small((length, 4 * wide)), small(rate.shape), small(taps.shape)],
        out_shape=[
            jax.ShapeDtypeStruct((length, 4 * wide), HALF),
            jax.ShapeDtypeStruct(rate.shape, SINGLE),
            jax.ShapeDtypeStruct(taps.shape, SINGLE),
        ],
        scratch_shapes=[pltpu.VMEM((length, wide), SINGLE)],
        compiler_params=pltpu.CompilerParams(vmem_limit_bytes=60 * 1024 * 1024),
        cost_estimate=pl.CostEstimate(flops=12000000000, bytes_accessed=8000000, transcendentals=0),
        name="attend_back",
    )(qkv, w, raw, rate, taps, marks, segc, segr, grads, tri, carried, probs)


def leave_kernel(part, half, *refs):
    place_ref, rows_ref, gain_ref = refs[:3]
    group_refs = refs[3:7]
    own_refs = refs[7:11]
    other_refs = refs[11:15]
    attended_ref, middle_ref, normed_ref = refs[15:]
    for i in range(4):
        at = pl.multiple_of(place_ref[i] * part, part)
        attended_ref[:, pl.ds(at, part)] = group_refs[i][...]
    own_at = pl.multiple_of(place_ref[4], half)
    other_at = pl.multiple_of(half - place_ref[4], half)
    for at, pieces in ((own_at, own_refs), (other_at, other_refs)):
        total = mm(attended_ref[:, :part], pieces[0][...])
        for r in range(1, 4):
            total = total + mm(attended_ref[:, r * part : (r + 1) * part], pieces[r][...])
        middle_ref[:, pl.ds(at, half)] = rows_ref[:, pl.ds(at, half)] + total
    middle = middle_ref[...]
    inverse = lax.rsqrt(jnp.mean(middle * middle, axis=-1, keepdims=True) + EPS)
    normed_ref[...] = (middle * inverse * gain_ref[...]).astype(HALF)


def leave_attention(places, rows, gain, groups, own, other):
    length, width = rows.shape
    vmem = pl.BlockSpec(memory_space=pltpu.VMEM)
    return pl.pallas_call(
        functools.partial(leave_kernel, width // 4, width // 2),
        in_specs=[pl.BlockSpec(memory_space=pltpu.SMEM)] + [vmem] * 14,
        out_specs=[vmem] * 3,
        out_shape=[
            jax.ShapeDtypeStruct((length, width), HALF),
            jax.ShapeDtypeStruct((length, width), SINGLE),
            jax.ShapeDtypeStruct((length, width), HALF),
        ],
        compiler_params=pltpu.CompilerParams(vmem_limit_bytes=60 * 1024 * 1024),
        cost_estimate=pl.CostEstimate(flops=6000000000, bytes_accessed=14000000, transcendentals=0),
        name="leave_attention",
    )(places, rows, gain, *groups, *own, *other)


def return_kernel(part, half, *refs):
    place_ref, own_ref, last_ref, upstream_ref, middle_ref, gain_ref = refs[:6]
    own_refs = refs[6:10]
    other_refs = refs[10:14]
    middle_grad_ref, branch_ref, gain_grad_ref, group_ref = refs[14:]
    middle = middle_ref[...]
    inverse = lax.rsqrt(jnp.mean(middle * middle, axis=-1, keepdims=True) + EPS)
    unit = middle * inverse
    grad = own_ref[...] + last_ref[...].astype(SINGLE)
    gain_grad_ref[...] = jnp.sum(grad * unit, axis=0, keepdims=True)
    scaled = grad * gain_ref[...]
    middle_grad_ref[...] = upstream_ref[...].astype(SINGLE) + inverse * (
        scaled - unit * jnp.mean(scaled * unit, axis=-1, keepdims=True)
    )
    own_at = pl.multiple_of(place_ref[4], half)
    other_at = pl.multiple_of(half - place_ref[4], half)
    branch_ref[:, :half] = middle_grad_ref[:, pl.ds(own_at, half)].astype(HALF)
    branch_ref[:, half:] = middle_grad_ref[:, pl.ds(other_at, half)].astype(HALF)
    for r in range(4):
        total = mm_nt(branch_ref[:, :half], own_refs[r][...]) + mm_nt(branch_ref[:, half:], other_refs[r][...])
        group_ref[place_ref[5 + r]] = total.astype(HALF)


def return_to_attention(places, own_sum, last, upstream, middle, gain, own, other):
    length, width = middle.shape
    vmem = pl.BlockSpec(memory_space=pltpu.VMEM)
    return pl.pallas_call(
        functools.partial(return_kernel, width // 4, width // 2),
        in_specs=[pl.BlockSpec(memory_space=pltpu.SMEM)] + [vmem] * 13,
        out_specs=[vmem] * 4,
        out_shape=[
            jax.ShapeDtypeStruct((length, width), SINGLE),
            jax.ShapeDtypeStruct((length, width), HALF),
            jax.ShapeDtypeStruct((1, width), SINGLE),
            jax.ShapeDtypeStruct((4, length, width // 4), HALF),
        ],
        compiler_params=pltpu.CompilerParams(vmem_limit_bytes=60 * 1024 * 1024),
        cost_estimate=pl.CostEstimate(flops=6000000000, bytes_accessed=14000000, transcendentals=0),
        name="return_to_attention",
    )(places, own_sum, last, upstream, middle, gain, *own, *other)


def feed_forward_kernel(units, rows_ref, feed_ref, down_ref, both_ref, hidden_ref, part_ref):
    both_ref[...] = mm(rows_ref[...], feed_ref[...])
    gate = both_ref[:, :units]
    hidden_ref[...] = (gate * jax.nn.sigmoid(gate) * both_ref[:, units:]).astype(HALF)
    part_ref[...] = mm(hidden_ref[...], down_ref[...]).astype(HALF)


def feed_forward(rows, mat_feed, mat_down, blocks):
    total, width = rows.shape
    units = mat_down.shape[0]
    size = total // blocks
    by_rows = lambda columns: pl.BlockSpec((size, columns), lambda i: (i, 0))
    whole = lambda a: pl.BlockSpec(a.shape, lambda i: (0, 0))
    return pl.pallas_call(
        functools.partial(feed_forward_kernel, units),
        grid=(blocks,),
        in_specs=[by_rows(width), whole(mat_feed), whole(mat_down)],
        out_specs=[by_rows(2 * units), by_rows(units), by_rows(width)],
        out_shape=[
            jax.ShapeDtypeStruct((total, 2 * units), SINGLE),
            jax.ShapeDtypeStruct((total, units), HALF),
            jax.ShapeDtypeStruct((total, width), HALF),
        ],
        compiler_params=pltpu.CompilerParams(vmem_limit_bytes=60 * 1024 * 1024),
        cost_estimate=pl.CostEstimate(flops=18000000000, bytes_accessed=30000000, transcendentals=0),
        name="feed_forward",
    )(rows, mat_feed, mat_down)


def feed_backward_kernel(units, *refs):
    upstream_ref, both_ref, feed_ref, down_ref = refs[:4]
    rows_ref, part_ref = refs[-2:]
    grad = mm_nt(upstream_ref[...], down_ref[...])
    gate = both_ref[:, :units]
    up = both_ref[:, units:]
    sig = jax.nn.sigmoid(gate)
    rows_ref[:, units:] = (grad * gate * sig).astype(HALF)
    rows_ref[:, :units] = (grad * up * sig * (1.0 + gate * (1.0 - sig))).astype(HALF)
    part_ref[...] = mm_nt(rows_ref[...], feed_ref[...]).astype(HALF)


def feed_backward(upstream, both, mat_feed, mat_down, blocks, first, number, filled=None):
    total, width = upstream.shape
    units = mat_down.shape[0]
    size = total // blocks
    by_rows = lambda columns: pl.BlockSpec((size, columns), lambda i: (i + first, 0))
    whole = lambda a: pl.BlockSpec(a.shape, lambda i: (0, 0))
    more = [] if filled is None else [filled]
    return pl.pallas_call(
        functools.partial(feed_backward_kernel, units),
        grid=(number,),
        in_specs=[by_rows(width), by_rows(2 * units), whole(mat_feed), whole(mat_down)]
        + [pl.BlockSpec(memory_space=pl.ANY)] * len(more),
        out_specs=[by_rows(2 * units), pl.BlockSpec((size, width), lambda i: (i, 0))],
        out_shape=[
            jax.ShapeDtypeStruct((total, 2 * units), HALF),
            jax.ShapeDtypeStruct((size * number, width), HALF),
        ],
        input_output_aliases={4: 0} if more else {},
        compiler_params=pltpu.CompilerParams(vmem_limit_bytes=60 * 1024 * 1024),
        cost_estimate=pl.CostEstimate(flops=9000000000, bytes_accessed=25000000, transcendentals=0),
        name="feed_backward",
    )(upstream, both, mat_feed, mat_down, *more)


AXES = ("grp", "fsdp")


def tie(*values):
    return lax.optimization_barrier(values)


def cut(array, start, size, axis):
    return lax.dynamic_slice_in_dim(array, start, size, axis)


def wide_sum(*terms):
    total = terms[0].astype(SINGLE)
    for term in terms[1:]:
        total = total + term.astype(SINGLE)
    return total


def turned(doc_row, taps_count):
    length = doc_row.shape[0]
    span = length // 2
    start = jnp.argmax(doc_row[: length - span + 1] == doc_row[span - 1 :])
    position = lax.iota(jnp.int32, length)
    source = (position + start) % length
    turn = (source[:, None] == position[None, :]).astype(HALF)
    segment = jnp.sum(jnp.where(turn > 0, doc_row[None, :], 0), axis=1)
    marks = jnp.stack(
        [((jnp.roll(segment, k) == segment) & (position >= k)).astype(SINGLE) for k in range(taps_count)],
        axis=1,
    )
    return turn, marks, segment[:, None], segment[None, :]


def turn_back(turn, array):
    high = array.astype(HALF)
    low = (array - high.astype(SINGLE)).astype(HALF)
    return mm_tn(turn, high) + mm_tn(turn, low)


def unit_norm(array):
    inverse = lax.rsqrt(jnp.mean(array * array, axis=-1, keepdims=True) + EPS)
    return array * inverse, inverse


def unit_back(grad, unit, inverse, gain):
    scaled = grad * gain
    return inverse * (scaled - unit * jnp.mean(scaled * unit, axis=-1, keepdims=True))


def gates(gate_rows, up_rows):
    gate_sig = jax.nn.sigmoid(gate_rows)
    return gate_sig, (gate_rows * gate_sig * up_rows).astype(HALF)


def gates_back(grad_hidden, gate_rows, up_rows, gate_sig):
    return jnp.concatenate(
        [
            (grad_hidden * up_rows * gate_sig * (1.0 + gate_rows * (1.0 - gate_sig))).astype(HALF),
            (grad_hidden * gate_rows * gate_sig).astype(HALF),
        ],
        axis=1,
    )


def local_any(
    tokens, doc_ids, cotangent, gain_in, w_query, w_key, w_value, w_house, w_rate, conv_taps, w_out,
    gain_mid, w_gate, w_up, w_down,
):
    heads = w_rate.shape[1]
    width = tokens.shape[2]
    dim = width // heads
    span = tokens.shape[1] // 2
    count = heads // 4
    wide = count * dim

    def fetch(array, axis=0):
        return lax.all_gather(array.astype(HALF), "fsdp", axis=axis, tiled=True)

    def share(array, axis=0):
        part = lax.psum_scatter(array.astype(HALF), "fsdp", scatter_dimension=axis, tiled=True)
        return lax.psum(part, "grp").astype(SINGLE)

    gain_first = fetch(gain_in).astype(SINGLE)
    gain_second = fetch(gain_mid).astype(SINGLE)
    projections = [fetch(w) for w in (w_query, w_key, w_value, w_house)]
    mat_rate = fetch(w_rate)
    tap_values = fetch(conv_taps, 1).astype(SINGLE)
    mat_out, mat_gate, mat_up, mat_down = [fetch(w) for w in (w_out, w_gate, w_up, w_down)]
    turn, marks, segc, segr = turned(doc_ids[0], conv_taps.shape[0])
    rows = mm(turn, tokens[0])
    upstream = mm(turn, cotangent[0]).astype(HALF)
    unit_in, inverse_in = unit_norm(rows)
    normed = (unit_in * gain_first).astype(HALF)
    rate_sig = jax.nn.sigmoid(
        lax.dot_general(mat_rate, normed, (((0,), (1,)), ((), ())), preferred_element_type=SINGLE)
    )
    rates = [2.0 * rate_sig[k * count : (k + 1) * count] for k in range(4)]
    taps = [tap_values[:, k * wide : (k + 1) * wide] for k in range(4)]
    pieces = [
        jnp.concatenate([w[:, k * wide : (k + 1) * wide] for w in projections], axis=1) for k in range(4)
    ]
    kept = [
        attn_forward(normed, [pieces[k]], rates[k], taps[k], marks, segc, segr, dim, span) for k in range(4)
    ]
    attended = jnp.concatenate([k[0] for k in kept], axis=1)
    middle = rows + mm(attended, mat_out)
    unit_mid, inverse_mid = unit_norm(middle)
    normed_mid = (unit_mid * gain_second).astype(HALF)
    gate_rows = mm(normed_mid, mat_gate)
    up_rows = mm(normed_mid, mat_up)
    gate_sig, hidden = gates(gate_rows, up_rows)
    result = (middle + mm(hidden, mat_down)).astype(HALF)
    feed_rows = gates_back(mm_nt(upstream, mat_down), gate_rows, up_rows, gate_sig)
    units = feed_rows.shape[1] // 2
    grad_gate_rows, grad_up_rows = feed_rows[:, :units], feed_rows[:, units:]
    grad_normed_mid = mm_nt(grad_gate_rows, mat_gate) + mm_nt(grad_up_rows, mat_up)
    grad_middle = upstream.astype(SINGLE) + unit_back(grad_normed_mid, unit_mid, inverse_mid, gain_second)
    grad_branch = grad_middle.astype(HALF)
    grad_att = mm_nt(grad_branch, mat_out).astype(HALF)
    row_grads, rate_grads, tap_grads = [], [], []
    for k in range(4):
        unused_out, qkv, raw, house, tri, carried, probs = kept[k]
        got = attn_backward(
            qkv, house, raw, rates[k], taps[k], marks, segc, segr, grad_att[None, :, k * wide : (k + 1) * wide], 0,
            tri, carried, probs, dim, span,
        )
        row_grads.append(got[0])
        rate_grads.append(got[1])
        tap_grads.append(got[2])
    grad_rate_rows = (jnp.concatenate(rate_grads, axis=0) * 2.0 * rate_sig * (1.0 - rate_sig)).astype(HALF)
    grad_normed = lax.dot_general(
        grad_rate_rows, mat_rate, (((0,), (1,)), ((), ())), preferred_element_type=SINGLE
    )
    for k in range(4):
        grad_normed = grad_normed + mm_nt(row_grads[k], pieces[k])
    grad_tokens = grad_middle + unit_back(grad_normed, unit_in, inverse_in, gain_first)
    weight_grads = []
    for m in range(4):
        part = jnp.concatenate([r[:, m * wide : (m + 1) * wide] for r in row_grads], axis=1)
        weight_grads.append(share(mm_tn(normed, part)))
    return (
        mm_tn(turn, result).astype(HALF)[None],
        turn_back(turn, grad_tokens)[None],
        share(jnp.sum(grad_normed * unit_in, axis=0)),
        weight_grads[0],
        weight_grads[1],
        weight_grads[2],
        weight_grads[3],
        share(lax.dot_general(normed, grad_rate_rows, (((0,), (1,)), ((), ())), preferred_element_type=SINGLE)),
        share(jnp.concatenate(tap_grads, axis=1), 1),
        share(mm_tn(attended, grad_branch)),
        share(jnp.sum(grad_normed_mid * unit_mid, axis=0)),
        share(mm_tn(normed_mid, grad_gate_rows)),
        share(mm_tn(normed_mid, grad_up_rows)),
        share(mm_tn(hidden, upstream)),
    )


class Links:
    def __init__(self, groups, shards):
        self.core = lax.axis_index("grp") % 2
        self.me = lax.axis_index("fsdp")
        near = 1 + self.core
        self.order = [self.me, self.me ^ near, self.me ^ (3 - near), self.me ^ 3]

        def permutation(move):
            pairs = []
            for g in range(groups):
                for f in range(shards):
                    target = move(g // 2, g % 2, f)
                    if target is not None:
                        pairs.append((g * shards + f, target[0] * shards + target[1]))
            return pairs

        self.pairs = {
            "near": permutation(lambda z, c, f: (2 * z + c, f ^ (1 + c))),
            "next": permutation(lambda z, c, f: (2 * z + c, f ^ (2 - c))),
            "twin": permutation(lambda z, c, f: (2 * z + 1 - c, f)),
            "far": permutation(lambda z, c, f: (2 * z + c, f ^ 3)),
            "level": permutation(lambda z, c, f: (2 * (z ^ 1) + c, f)),
            "pair": permutation(lambda z, c, f: (2 * (3 - z) + c, f)),
            "inward": permutation(lambda z, c, f: (2 * (z ^ 1) + c, f) if z in (0, 3) else None),
            "across": permutation(lambda z, c, f: (2 * (3 - z) + c, f) if z in (1, 2) else None),
            "outward": permutation(lambda z, c, f: (2 * (z ^ 1) + c, f) if z in (1, 2) else None),
        }
        level = lax.axis_index("grp") // 2
        self.edge = (level == 0) | (level == 3)
        self.keep = jnp.where(self.edge, 0, 1)
        self.columns = [[2 * z + c for z in range(groups // 2)] for c in range(2)]

    def near(self, array):
        return lax.ppermute(array, AXES, self.pairs["near"])

    def next(self, array):
        return lax.ppermute(array, AXES, self.pairs["next"])

    def twin(self, array):
        return lax.ppermute(array, AXES, self.pairs["twin"])

    def far(self, array):
        return lax.ppermute(array, AXES, self.pairs["far"])

    def level(self, array):
        return lax.ppermute(array, AXES, self.pairs["level"])

    def pair(self, array):
        return lax.ppermute(array, AXES, self.pairs["pair"])

    def inward(self, array):
        return lax.ppermute(array, AXES, self.pairs["inward"])

    def across(self, array):
        return lax.ppermute(array, AXES, self.pairs["across"])

    def outward(self, array):
        return lax.ppermute(array, AXES, self.pairs["outward"])

    def settled(self, total, got):
        return jnp.where(self.edge, got, total)

    def halves(self, array, axis):
        pick = lambda i: lax.dynamic_index_in_dim(array, i, axis, keepdims=False)
        return pick(self.keep), pick(1 - self.keep)

    def joined(self, mine, partner, axis):
        return jnp.where(
            self.edge, jnp.stack([mine, partner], axis=axis), jnp.stack([partner, mine], axis=axis)
        )

    def place(self, number):
        apart = number ^ self.me
        return jnp.where((apart == 0) | (apart == 3) | (self.core == 0), apart, 3 - apart)

    def in_place(self, blocks):
        rows = blocks[0].shape[0]
        every = jnp.zeros((rows * 4,) + blocks[0].shape[1:], blocks[0].dtype)
        for number, block in zip(self.order, blocks):
            every = lax.dynamic_update_slice(every, block, (number * rows,) + (0,) * (block.ndim - 1))
        return every

    def by_core(self, own, other, axis):
        return jnp.where(
            self.core == 0,
            jnp.concatenate([own, other], axis=axis),
            jnp.concatenate([other, own], axis=axis),
        )


def core_sum(own, got):
    rows = own.shape[0] // 4
    flip = [got[i * rows : (i + 1) * rows] for i in (0, 2, 1, 3)]
    head = wide_sum(own[: 2 * rows], jnp.concatenate(flip[:2], axis=0)).astype(HALF)
    tail = wide_sum(own[2 * rows :], jnp.concatenate(flip[2:], axis=0)).astype(HALF)
    return head, tail


def second_sum(head, got):
    rows = head.shape[0] // 2
    return wide_sum(head[:rows], got[:rows]), wide_sum(head[rows:], got[rows:]).astype(HALF)


def local_paired(
    tokens, doc_ids, cotangent, gain_in, w_query, w_key, w_value, w_house, w_rate, conv_taps, w_out,
    gain_mid, w_gate, w_up, w_down, *, groups, shards,
):
    links = Links(groups, shards)
    core = links.core
    length = tokens.shape[1]
    width = tokens.shape[2]
    span = length // 2
    heads = w_rate.shape[1]
    dim = width // heads
    taps_count = conv_taps.shape[0]
    part = width // shards
    half_width = width // 2
    count = heads // 4
    wide = count * dim
    own_at = core * half_width
    other_at = half_width - own_at
    number = [2 * core, 2 * core + 1, 2 - 2 * core, 3 - 2 * core]
    hidden_part = w_gate.shape[1] // shards
    h = hidden_part // 2
    hid_own = core * h
    hid_other = h - hid_own

    def group_columns(k):
        return jnp.concatenate(
            [cut(matrix, k * wide, wide, 1).astype(HALF) for matrix in (w_query, w_key, w_value, w_house)],
            axis=1,
        )

    def feed_block(i):
        start = i * hidden_part + hid_own
        return jnp.concatenate([cut(w_gate, start, h, 1), cut(w_up, start, h, 1)], axis=1).astype(HALF)

    def in_order(array, axis):
        return jnp.concatenate([cut(array, i * part, part, axis) for i in links.order], axis=axis)

    def from_order(array, axis):
        return jnp.concatenate([cut(array, links.place(i) * part, part, axis) for i in range(4)], axis=axis)

    small = jnp.concatenate([gain_in[:, None], gain_mid[:, None], conv_taps.T, w_rate], axis=1).astype(HALF)
    small = jnp.pad(small, ((0, 0), (0, 128 - small.shape[1])))
    small_near, small_second, small_far = links.near(small), links.next(small), links.far(small)
    block0 = group_columns(number[0])
    near0, second0 = links.near(block0), links.next(block0)

    turn, marks, segc, segr = turned(doc_ids[0], taps_count)
    rows = mm(turn, tokens[0])
    unit_in, inverse_in = unit_norm(rows)
    unit_in = in_order(unit_in, 1)
    block1 = group_columns(number[1])

    near0, second0, small_near, small_second, small_far, block1, unit_in = tie(
        near0, second0, small_near, small_second, small_far, block1, unit_in
    )
    far0 = links.next(near0)
    twin0 = [links.twin(second0), links.twin(near0)]
    small = [small, small_near, small_second, small_far]
    small_order = jnp.concatenate(small, axis=0)
    small_plain = links.in_place(small)
    gain_first = small_order[:, 0].astype(SINGLE)
    gain_second = small_plain[:, 1].astype(SINGLE)
    tap_values = small_plain[:, 2 : 2 + taps_count].astype(SINGLE)
    mat_rate = small_order[:, 2 + taps_count : 2 + taps_count + heads]
    normed = (unit_in * gain_first).astype(HALF)
    rate_sig = jax.nn.sigmoid(
        lax.dot_general(mat_rate, normed, (((0,), (1,)), ((), ())), preferred_element_type=SINGLE)
    )
    rates = [cut(2.0 * rate_sig, k * count, count, 0) for k in number]
    taps = [cut(tap_values, k * wide, wide, 0).T for k in number]
    normed, far0, block1, *rest = tie(normed, far0, block1, *rates, *taps)
    rates, taps = rest[:4], rest[4:]

    def forward(i, normed, pieces):
        return attn_forward(normed, pieces, rates[i], taps[i], marks, segc, segr, dim, span)

    kept = [None] * 4
    pieces = [None] * 4
    pieces[0] = [block0, near0, second0, far0]
    twin0.append(links.twin(far0))
    near1, second1 = links.near(block1), links.next(block1)
    kept[0] = forward(0, normed, pieces[0])
    block2 = group_columns(number[2])
    out_block = cut(w_out, own_at, half_width, 1).astype(HALF)

    normed, unused, near1, second1, out_block, block2, *twin0 = tie(
        normed, kept[0][0], near1, second1, out_block, block2, *twin0
    )
    far1 = links.next(near1)
    twin1 = [links.twin(second1), links.twin(near1)]
    pieces[2] = [block2] + twin0
    kept[2] = forward(2, normed, pieces[2])
    block3 = group_columns(number[3])
    out_rest = cut(w_out, other_at, half_width, 1).astype(HALF)

    far1, normed, unused, out_block, block3, out_rest = tie(far1, normed, kept[2][0], out_block, block3, out_rest)
    twin1.append(links.twin(far1))
    pieces[1] = [block1, near1, second1, far1]
    out_near, out_second = links.near(out_block), links.next(out_block)
    kept[1] = forward(1, normed, pieces[1])
    feed_first, feed_second, feed_far = [feed_block(i) for i in links.order[1:]]
    upstream = mm(turn, cotangent[0]).astype(HALF)

    normed, unused, out_near, out_second, feed_first, feed_second, feed_far, upstream, *twin1 = tie(
        normed, kept[1][0], out_near, out_second, feed_first, feed_second, feed_far, upstream, *twin1
    )
    pieces[3] = [block3] + twin1
    out_far = links.next(out_near)
    feed_passing = links.near(feed_far)
    feed_near = links.near(feed_first)
    feed_next = links.next(feed_second)
    out_twin = [links.twin(out_second), links.twin(out_near)]
    kept[3] = forward(3, normed, pieces[3])

    att3, out_far, feed_passing, *out_twin = tie(kept[3][0], out_far, feed_passing, *out_twin)
    feed_last = links.next(feed_passing)
    up_near, up_second = links.near(upstream), links.next(upstream)
    out_twin.append(links.twin(out_far))
    places = [links.place(k) for k in number] + [own_at] + [k ^ (2 * core) for k in links.order]
    places = jnp.stack([jnp.asarray(p, jnp.int32) for p in places])
    gain_second = gain_second[None, :]
    out_own = [out_block, out_near, out_second, out_far]
    out_other = [out_rest] + out_twin
    attended, middle, normed_mid = leave_attention(
        places, rows, gain_second, [kept[0][0], kept[1][0], kept[2][0], att3], out_own, out_other
    )

    normed_mid, feed_near, feed_next, up_near, up_second = tie(
        normed_mid, feed_near, feed_next, up_near, up_second
    )

    mid_near, mid_second = links.near(normed_mid), links.next(normed_mid)
    feed_mine = feed_block(links.me)
    mat_down = jnp.concatenate(
        [cut(w_down, hid_own, h, 0), cut(w_down, hid_other, h, 0)], axis=0
    ).astype(HALF)
    mid_near, mid_second, feed_mine, mat_down = tie(mid_near, mid_second, feed_mine, mat_down)
    mid_far = links.next(mid_near)
    feed_own = links.in_place([feed_mine, feed_near, feed_next, feed_last])
    feed_other = links.twin(feed_own)
    mat_feed = jnp.concatenate(
        [feed_own[:, :h], feed_other[:, :h], feed_own[:, h:], feed_other[:, h:]], axis=1
    )
    mat_feed, mid_far, up_near = tie(mat_feed, mid_far, up_near)
    up_far = links.next(up_near)
    normed_all = jnp.concatenate([normed_mid, mid_near, mid_second, mid_far], axis=0)
    gate_up, hidden, down_part = feed_forward(normed_all, mat_feed, mat_down, shards)
    up_far, gate_up, hidden = tie(up_far, gate_up, hidden)
    upstream_all = jnp.concatenate([upstream, up_near, up_second, up_far], axis=0)
    feed_rows, mid_tail = feed_backward(upstream_all, gate_up, mat_feed, mat_down, shards, 2, 2)

    mid_tail, feed_rows, hidden, upstream_all = tie(mid_tail, feed_rows, hidden, upstream_all)
    mid_got = links.next(mid_tail)
    grad_down = mm_tn(hidden, upstream_all).astype(HALF)
    grad_down, feed_rows, upstream_all = tie(grad_down, feed_rows, upstream_all)
    down_got = links.twin(grad_down[h:])
    feed_rows, mid_head = feed_backward(upstream_all, gate_up, mat_feed, mat_down, shards, 0, 2, feed_rows)
    mid_got, mid_head, down_got, feed_rows = tie(mid_got, mid_head, down_got, feed_rows)
    mid_own, mid_first = second_sum(mid_head, mid_got)
    mid_last = links.near(mid_first)
    down_sum = wide_sum(grad_down[:h], down_got).astype(HALF)
    down_in = links.inward(down_sum)
    grad_feed = mm_tn(normed_all, feed_rows).astype(HALF)

    mid_last, grad_feed, mid_own, down_part = tie(mid_last, grad_feed, mid_own, down_part)
    feed_got = links.twin(jnp.concatenate([grad_feed[:, h : 2 * h], grad_feed[:, 3 * h :]], axis=1))
    result_got = links.next(down_part[2 * length :])
    grad_middle, branch_pair, grad_gain_mid, grad_att = return_to_attention(
        places, mid_own, mid_last, upstream, middle, gain_second, out_own, out_other
    )
    out_grads = mm_tn(attended, branch_pair).astype(HALF)

    def backward(i, grad_att):
        unused_out, qkv, raw, house, tri, carried, probs = kept[i]
        return attn_backward(
            qkv, house, raw, rates[i], taps[i], marks, segc, segr, grad_att, i, tri, carried, probs, dim, span
        )

    row_grads = [None] * 4
    rate_grads = [None] * 4
    tap_grads = [None] * 4
    out_grads, feed_got, grad_att = tie(out_grads, feed_got, grad_att)
    out_got = links.twin(out_grads[:, half_width:])
    feed_sum = wide_sum(
        jnp.concatenate([grad_feed[:, :h], grad_feed[:, 2 * h : 3 * h]], axis=1), feed_got
    ).astype(HALF)
    feed0, feed1 = feed_sum[: width // 2], feed_sum[width // 2 :]
    row_grads[2], rate_grads[2], tap_grads[2] = backward(2, grad_att)
    other = mm_tn(normed, row_grads[2]).astype(HALF)

    other, out_got, grad_att, down_in, feed0, feed1, result_got = tie(
        other, out_got, grad_att, down_in, feed0, feed1, result_got
    )
    got0 = links.twin(other)
    feed0_in = links.inward(feed0)
    down_sum = wide_sum(down_sum, down_in).astype(HALF)
    down_across = links.across(down_sum)
    out_head, out_tail = core_sum(out_grads[:, :half_width], out_got)
    out_part = links.next(out_tail)
    result_own, result_first = second_sum(down_part[: 2 * length], result_got)
    result_last = links.near(result_first)
    row_grads[0], rate_grads[0], tap_grads[0] = backward(0, grad_att)
    own0 = mm_tn(normed, row_grads[0]).astype(HALF)

    own0, got0, out_part, grad_att = tie(own0, got0, out_part, grad_att)
    head0, tail0 = core_sum(own0, got0)
    part0 = links.next(tail0)
    out_own_sum, out_first = second_sum(out_head, out_part)
    out_last = links.near(out_first)
    row_grads[3], rate_grads[3], tap_grads[3] = backward(3, grad_att)
    other = mm_tn(normed, row_grads[3]).astype(HALF)

    other, out_last, grad_att, feed0_in, down_across, result_last = tie(
        other, out_last, grad_att, feed0_in, down_across, result_last
    )
    got1 = links.twin(other)
    feed1_in = links.inward(feed1)
    feed0 = wide_sum(feed0, feed0_in).astype(HALF)
    feed0_across = links.across(feed0)
    down_sum = wide_sum(down_sum, down_across).astype(HALF)
    down_out = links.outward(down_sum)
    out_sum = wide_sum(out_own_sum, out_last).astype(HALF)
    result = (middle + wide_sum(result_own, result_last)).astype(HALF)
    result = mm_tn(turn, result).astype(HALF)
    row_grads[1], rate_grads[1], tap_grads[1] = backward(1, grad_att)
    own1 = mm_tn(normed, row_grads[1]).astype(HALF)

    own1, got1, part0, out_sum, feed1_in, feed0_across, *late = tie(
        own1, got1, part0, out_sum, feed1_in, feed0_across, *row_grads
    )
    feed1 = wide_sum(feed1, feed1_in).astype(HALF)
    feed1_across = links.across(feed1)
    feed0 = wide_sum(feed0, feed0_across).astype(HALF)
    feed0_out = links.outward(feed0)
    sum0, first0 = second_sum(head0, part0)
    last0 = links.near(first0)
    head1, tail1 = core_sum(own1, got1)
    part1 = links.next(tail1)

    grad_rate = links.by_core(
        jnp.concatenate(rate_grads[:2], axis=0), jnp.concatenate(rate_grads[2:], axis=0), 0
    )
    grad_taps = links.by_core(
        jnp.concatenate(tap_grads[:2], axis=1), jnp.concatenate(tap_grads[2:], axis=1), 1
    )
    grad_rate_rows = (grad_rate * 2.0 * rate_sig * (1.0 - rate_sig)).astype(HALF)
    grad_wrate = lax.dot_general(
        normed, grad_rate_rows, (((0,), (1,)), ((), ())), preferred_element_type=SINGLE
    )
    grad_normed = lax.dot_general(
        grad_rate_rows, mat_rate, (((0,), (1,)), ((), ())), preferred_element_type=SINGLE
    )
    for i in (0, 2):
        grad_normed = grad_normed + mm_nt(late[i], jnp.concatenate(pieces[i], axis=0))

    last0, grad_normed, down_out, feed1_across, feed0_out = tie(
        last0, grad_normed, down_out, feed1_across, feed0_out
    )
    feed1 = wide_sum(feed1, feed1_across).astype(HALF)
    feed1_out = links.outward(feed1)
    out_in = links.inward(out_sum)
    sum0 = wide_sum(sum0, last0).astype(HALF)
    sum0_in = links.inward(sum0)
    down_sum = links.settled(down_sum, down_out)
    down_twin = links.twin(down_sum)
    for i in (1, 3):
        grad_normed = grad_normed + mm_nt(late[i], jnp.concatenate(pieces[i], axis=0))
    grad_gain_in = jnp.sum(grad_normed * unit_in, axis=0)
    extra = jnp.concatenate(
        [grad_gain_in[:, None], in_order(grad_gain_mid[0], 0)[:, None], in_order(grad_taps.T, 0), grad_wrate],
        axis=1,
    )
    extra = jnp.pad(extra, ((0, 0), (0, 128 - extra.shape[1]))).astype(HALF)

    extra, part1, out_in, grad_normed = tie(extra, part1, out_in, grad_normed)
    extra_got = links.twin(extra)
    sum1, first1 = second_sum(head1, part1)
    last1 = links.near(first1)
    out_sum = wide_sum(out_sum, out_in).astype(HALF)
    out_across = links.across(out_sum)
    norm_grad = unit_back(grad_normed, unit_in, inverse_in, gain_first)
    grad_tokens = turn_back(turn, grad_middle + from_order(norm_grad, 1))

    grad_tokens, sum0_in, extra_got, last1 = tie(grad_tokens, sum0_in, extra_got, last1)
    sum0 = wide_sum(sum0, sum0_in).astype(HALF)
    sum0_across = links.across(sum0)
    sum1 = wide_sum(sum1, last1).astype(HALF)
    sum1 = [sum1[: part // 2], sum1[part // 2 :]]
    sum1_in = [links.inward(a) for a in sum1]
    extra_head, extra_tail = core_sum(extra, extra_got)
    extra_part = links.next(extra_tail)
    grad_down = links.by_core(down_sum, down_twin, 0).astype(SINGLE)
    feed0 = links.settled(feed0, feed0_out)

    sum0_across, out_across, grad_down, extra_part = tie(sum0_across, out_across, grad_down, extra_part)
    extra_own, extra_first = second_sum(extra_head, extra_part)
    extra_last = links.near(extra_first)
    both0 = jnp.concatenate([wide_sum(sum0, sum0_across), wide_sum(out_sum, out_across)], axis=1).astype(HALF)
    both0_out = links.outward(both0)

    feed1_out, feed0, both0, extra_first, *sum1_in = tie(feed1_out, feed0, both0, extra_first, *sum1_in)
    sum1 = [wide_sum(a, b).astype(HALF) for a, b in zip(sum1, sum1_in)]
    sum1_across = [links.across(a) for a in sum1]
    feed_sum = jnp.concatenate([feed0, links.settled(feed1, feed1_out)], axis=0)
    feed_blocks = [cut(feed_sum, i * part, part, 0) for i in links.order]
    feed_passing, feed_near = links.near(feed_blocks[3]), links.near(feed_blocks[1])
    feed_next = links.next(feed_blocks[2])

    feed_passing, extra_last, *sum1_across = tie(feed_passing, extra_last, *sum1_across)
    feed_last = links.next(feed_passing)
    sum1 = [wide_sum(a, b).astype(HALF) for a, b in zip(sum1, sum1_across)]
    sum1_out = [links.outward(a) for a in sum1]
    extra_sum = wide_sum(extra_own, extra_last).astype(HALF)
    extra_level = links.level(extra_sum)

    feed_last, both0_out, extra_level, *sum1_out = tie(feed_last, both0_out, extra_level, *sum1_out)
    both0 = links.settled(both0, both0_out)
    both_twin = links.twin(both0)
    sum0, out_sum = both0[:, : 4 * wide], both0[:, 4 * wide :]
    twin0, out_twin = both_twin[:, : 4 * wide], both_twin[:, 4 * wide :]

    extra_sum = wide_sum(extra_sum, extra_level).astype(HALF)
    extra_pair = links.pair(extra_sum)
    grad_wout = links.by_core(out_sum, out_twin, 1).astype(SINGLE)

    feed_mine = links.in_place([feed_blocks[0], feed_near, feed_next, feed_last])
    feed_twin = links.twin(feed_mine)
    sum1 = jnp.concatenate([links.settled(a, b) for a, b in zip(sum1, sum1_out)], axis=0)
    twin1 = links.twin(sum1)
    extra = wide_sum(extra_sum, extra_pair)

    grad_gate, grad_up = [
        jnp.concatenate(
            [
                links.by_core(
                    feed_mine[i * part : (i + 1) * part, at : at + h],
                    feed_twin[i * part : (i + 1) * part, at : at + h],
                    1,
                )
                for i in range(shards)
            ],
            axis=1,
        ).astype(SINGLE)
        for at in (0, h)
    ]
    sums = [(sum0, twin0), (sum1, twin1)]
    weight_grads = []
    for m in range(4):
        columns = [[a[:, m * wide : (m + 1) * wide] for a in pair] for pair in sums]
        weight_grads.append(
            links.by_core(
                jnp.concatenate([columns[0][0], columns[1][0]], axis=1),
                jnp.concatenate([columns[0][1], columns[1][1]], axis=1),
                1,
            ).astype(SINGLE)
        )

    return (
        result[None],
        grad_tokens[None],
        extra[:, 0],
        weight_grads[0],
        weight_grads[1],
        weight_grads[2],
        weight_grads[3],
        extra[:, 2 + taps_count : 2 + taps_count + heads],
        extra[:, 2 : 2 + taps_count].T,
        grad_wout,
        extra[:, 1],
        grad_gate,
        grad_up,
        grad_down,
    )


def solution(mesh):
    groups, shards = mesh.shape["grp"], mesh.shape["fsdp"]
    if (groups, shards) == (8, 4):
        body = functools.partial(local_paired, groups=groups, shards=shards)
    else:
        body = local_any
    rows = P(("grp", "fsdp"), None, None)
    vector = P("fsdp")
    matrix = P("fsdp", None)
    taps = P(None, "fsdp")
    return jax.shard_map(
        body,
        mesh=mesh,
        in_specs=(
            rows, P(("grp", "fsdp"), None), rows, vector, matrix, matrix, matrix, matrix, matrix,
            taps, matrix, vector, matrix, matrix, matrix,
        ),
        out_specs=(
            rows, rows, vector, matrix, matrix, matrix, matrix, matrix, taps, matrix, vector,
            matrix, matrix, matrix,
        ),
        check_vma=False,
    )
```
